128 devices in a mesh: curve: 32 (over y, z, core), sub: 4 (over x).
Axes of the slice: x: 4, y: 4, z: 4, core: 2. Of those that a mesh axis runs over, the one named last changes fastest.
Arguments:
- prognostic: float32 [4, 768, 32, 4, 4, 128], P(None, 'curve', 'sub'), may hold values from -6 to 6
- layer_mass: float32 [768, 32, 4, 4, 128], P('curve', 'sub'), may hold values from 0.5 to 2
- column_aux: bfloat16 [196608, 1013], P(('curve', 'sub')), may hold values from -6 to 6
- group_owner: int32 [98304, 1], P(('curve', 'sub')), may hold values from 0 to 127; in each aligned block of 768 rows (0 to 767, 768 to 1535, ...) at most 12 rows name the same one
- weight_in: bfloat16 [1525, 2048], replicated, may hold values from -0.15625 to 0.15625
- bias_in: float32 [2048], replicated, may hold values from -3 to 3
- weight_out: bfloat16 [2048, 512], replicated, may hold values from -0.125 to 0.125
- bias_out: float32 [512], replicated, may hold values from -2 to 2
Outputs:
- advanced: float32 [4, 768, 32, 4, 4, 128], P(None, 'curve', 'sub')
The draws below stay inside these ranges and needn't reach their ends.
Inputs may be any that keep to these rules, and one draw needn't show every extreme that they name: `group_owner`: among the 768 columns of one device, at most 12 name the same owner, and every device owns some column.
All inputs are finite; a program needn't handle non-finite values.
Results may differ from the reference program's by a relative error of at most 0.0035.
Values may be sent and summed in bfloat16 or wider, within the bound.
A program may use at most 128 MiB of HBM per device.

```python
import math
import jax
import jax.numpy as jnp
import numpy as np
from jax import lax

NV = 4
LEV = 128
F_IN = 1525
HID = 2048
EA = 24
EB = 8
AUX = 1013
COL_DEV = 768
COLUMNS = 98304
CAP = 12
NEA = 768
NEB = 32
N_CURVE = 32
N_SUB = 4
DEVICES = 128


def level_of(key, dims, cuts, low, top_value):
    gain = 1.0
    for dim, blocks in cuts:
        heights = jax.random.uniform(jax.random.fold_in(jax.random.fold_in(key, 6), dim), (blocks,), jnp.float32, low / len(cuts), top_value / len(cuts))
        gain = gain * jnp.repeat(jnp.exp(heights), dims[dim] // blocks).reshape((-1,) + (1,) * (len(dims) - 1 - dim))
    return gain


def routed_block(rng, own, number, rows, number_of, top, bound, slope):
    order = jax.random.permutation(rng, number_of)
    packed, usual = shares(number_of, rows * top, bound, slope, True), shares(number_of, rows * top, bound, slope, False)
    places = jnp.arange(number_of)

    def named(sizes, offset_by):
        used = int((sizes > 0).sum())
        fixed = max(1, used // 4)
        shifted = fixed + (places - fixed + offset_by * (used - fixed)) % max(1, number_of - fixed)
        return jnp.zeros((number_of,), jnp.int32).at[order[jnp.where(places < fixed, places, shifted)]].set(jnp.asarray(sizes, jnp.int32))

    sizes = jnp.where(number % 4 == 0, named(packed, number // 4), named(usual, number - number // 4 - 1))
    mixed = jax.random.permutation(jax.random.fold_in(own, 3), number_of)
    donor, sink = mixed[0:number_of // 2 * 2:2], mixed[1:number_of // 2 * 2:2]
    room = jnp.minimum(sizes[donor] - 1, bound - sizes[sink]) // 2
    room = jnp.where((donor == order[0]) | (sink == order[0]) | (sizes[sink] == 0), 0, jnp.maximum(room, 0))
    shifted = jax.random.randint(jax.random.fold_in(own, 4), (number_of // 2,), 0, 1 << 20) % (room + 1)
    sizes = sizes.at[donor].add(-shifted).at[sink].add(shifted)
    members = jnp.searchsorted(jnp.cumsum(sizes), jnp.arange(rows * top), side="right").astype(jnp.int32)
    grid = members.reshape(top, rows).T
    grid = grid[jax.random.permutation(jax.random.fold_in(own, 1), rows)]
    offset_by = jax.random.randint(jax.random.fold_in(own, 2), (rows, 1), 0, top)
    return jnp.take_along_axis(grid, (jnp.arange(top)[None, :] + offset_by) % top, axis=1)


def shares(count, total, most, skew, full):
    portions = [(1 << 20) // math.isqrt(rank ** skew) + 1 for rank in range(1, count + 1)]
    largest = most if full else min(most, max(-(-total // count), total * portions[0] // sum(portions)))
    least = 1 if total - largest >= count - 1 else 0
    holding, rest = [largest] + [least] * (count - 1), total - largest - least * (count - 1)
    while rest > 0:
        candidates = [i for i in range(1, count) if holding[i] < largest] or [i for i in range(1, count) if holding[i] < most]
        whole, budget = sum([portions[i] for i in candidates]), rest
        for i in candidates:
            extra = min(most - holding[i], max(1, budget * portions[i] // whole), rest)
            holding[i] = holding[i] + extra
            rest = rest - extra
    return np.array(holding)


def bell_draw(rng, dims, spread, reach, cuts=(), kind=jnp.bfloat16):
    factor_of = level_of(rng, dims, cuts, -0.22, 0.18) if cuts else 1.0
    result = jax.random.normal(rng, dims, jnp.float32) * spread * factor_of
    return jnp.minimum(jnp.maximum(result, -reach), reach).astype(kind)


def setup_inputs(seed: int = 0) -> dict:
    streams_of = jax.random.split(jax.random.key(seed), 9)
    prognostic = bell_draw(streams_of[0], (NV, NEA, NEB, 4, 4, LEV), 1.0, 6.0, ((1, 32), (2, 4)), jnp.float32)
    layer_mass = jnp.clip(jnp.exp(math.log(2.0) - 1.3862944 * jax.random.uniform(streams_of[1], (NEA, NEB, 4, 4, LEV), jnp.float32) ** level_of(streams_of[1], (NEA, NEB, 4, 4, LEV), ((0, 32), (1, 4)), -0.2, 0.2)), 0.5, 2.0)
    column_aux = bell_draw(streams_of[2], (DEVICES * DEVICES * CAP, AUX), 1.0, 6.0, ((0, 128),))
    group_owner_keys = jax.random.split(jax.random.fold_in(streams_of[3], 1), COLUMNS // COL_DEV)
    group_owner_turns = jax.random.permutation(jax.random.fold_in(streams_of[3], 3), COLUMNS // COL_DEV)
    group_owner = jax.vmap(lambda own, number: routed_block(jax.random.fold_in(streams_of[3], 2), own, number, COL_DEV, DEVICES, 1, CAP, 2))(group_owner_keys, group_owner_turns).reshape((COLUMNS, 1))
    weight_in = bell_draw(streams_of[4], (F_IN, HID), F_IN ** -0.5, 0.15625)
    bias_in = bell_draw(streams_of[5], (HID,), 0.5, 3.0, (), jnp.float32)
    weight_out = bell_draw(streams_of[6], (HID, NV * LEV), HID ** -0.5, 0.125)
    bias_out = bell_draw(streams_of[7], (NV * LEV,), 0.3, 2.0, (), jnp.float32)
    return {"prognostic": prognostic, "layer_mass": layer_mass, "column_aux": column_aux, "group_owner": group_owner, "weight_in": weight_in, "bias_in": bias_in, "weight_out": weight_out, "bias_out": bias_out}


section_step = 0.1

def node_tables():
    nodes = np.array([-1.0, -1.0 / np.sqrt(5.0), 1.0 / np.sqrt(5.0), 1.0])
    quadrature = np.array([1.0 / 6.0, 5.0 / 6.0, 5.0 / 6.0, 1.0 / 6.0])
    products = np.array([np.prod([nodes[left_node] - nodes[other_node] for other_node in range(4) if other_node != left_node]) for left_node in range(4)])
    derivative = np.zeros((4, 4))
    for left_node in range(4):
        for other_node in range(4):
            if left_node != other_node:
                derivative[left_node, other_node] = products[left_node] / (products[other_node] * (nodes[left_node] - nodes[other_node]))
            else:
                derivative[left_node, left_node] = sum((1.0 / (nodes[left_node] - nodes[third_node]) for third_node in range(4) if third_node != left_node))
    return (derivative.astype(np.float32), quadrature.astype(np.float32))

def advect(prognostic, derivative):
    along_first = jnp.einsum('ik,fabkjl->fabijl', derivative, prognostic, precision=lax.Precision.HIGHEST)
    along_second = jnp.einsum('jk,fabikl->fabijl', derivative, prognostic, precision=lax.Precision.HIGHEST)
    return -(prognostic[0:1] * along_first + prognostic[1:2] * along_second)

def node_mass(layer_mass, quadrature):
    return quadrature[:, None, None] * quadrature[None, :, None] * layer_mass

def cell_average(prognostic, node_weight):
    fields = prognostic.shape[0]
    rows_a, rows_b, levels = (node_weight.shape[0], node_weight.shape[1], node_weight.shape[4])
    weighted = (prognostic * node_weight[None]).reshape(fields, rows_a, rows_b, 2, 2, 2, 2, levels)
    weighted_sum = lax.optimization_barrier(jnp.sum(weighted, axis=(4, 6)))
    mass_sum = lax.optimization_barrier(jnp.sum(node_weight.reshape(rows_a, rows_b, 2, 2, 2, 2, levels), axis=(3, 5)))
    return weighted_sum / mass_sum[None]

def spread_cells(cells):
    return jnp.repeat(jnp.repeat(cells, 2, axis=3), 2, axis=4)

def apply_network(inputs, weight_in, bias_in, weight_out, bias_out):
    hidden = jax.nn.silu(jnp.dot(inputs, weight_in, preferred_element_type=jnp.float32) + bias_in).astype(jnp.bfloat16)
    return (jnp.dot(hidden, weight_out, preferred_element_type=jnp.float32) + bias_out).astype(jnp.bfloat16)

def reference(prognostic, layer_mass, column_aux, group_owner, weight_in, bias_in, weight_out, bias_out):
    derivative_np, quadrature_np = node_tables()
    derivative = jnp.asarray(derivative_np)
    quadrature = jnp.asarray(quadrature_np)
    advection = advect(prognostic, derivative)
    node_weight = node_mass(layer_mass, quadrature)
    stacked = jnp.concatenate([advection * node_weight[None], node_weight[None]], axis=0)
    following = jnp.roll(stacked, -1, axis=1)
    preceding = jnp.roll(stacked, 1, axis=1)
    passed = stacked.at[:, :, :, 3].add(following[:, :, :, 0]).at[:, :, :, 0].add(preceding[:, :, :, 3])
    following = jnp.roll(passed, -1, axis=2)
    preceding = jnp.roll(passed, 1, axis=2)
    summed = passed.at[:, :, :, :, 3].add(following[:, :, :, :, 0]).at[:, :, :, :, 0].add(preceding[:, :, :, :, 3])
    section = prognostic + section_step * (summed[:NV] / summed[NV:])
    cells = cell_average(prognostic, node_weight)
    state_cols = cells.reshape(NV, N_CURVE, EA, N_SUB, EB, 2, 2, LEV).transpose(1, 3, 2, 4, 5, 6, 0, 7)
    state_cols = state_cols.reshape(COLUMNS, NV * LEV).astype(jnp.bfloat16)
    targets = group_owner[:, 0].reshape(DEVICES, COL_DEV)
    hits = (targets[:, :, None] == jnp.arange(DEVICES, dtype=jnp.int32)[None, None]).astype(jnp.int32)
    earlier = (jnp.cumsum(hits, axis=1) - hits).astype(jnp.int32)
    slot_index = lax.optimization_barrier(jnp.sum(hits * earlier, axis=2)).astype(jnp.int32)
    source = jnp.arange(DEVICES, dtype=jnp.int32)[:, None]
    aux_rows = (targets * (DEVICES * CAP) + source * CAP + slot_index).reshape(COLUMNS).astype(jnp.int32)
    aux_cols = column_aux[aux_rows]
    increment = apply_network(jnp.concatenate([state_cols, aux_cols], axis=1), weight_in, bias_in, weight_out, bias_out)
    back = increment.reshape(N_CURVE, N_SUB, EA, EB, 2, 2, NV, LEV).transpose(6, 0, 2, 1, 3, 4, 5, 7)
    back = back.reshape(NV, NEA, NEB, 2, 2, LEV)
    return section + spread_cells(back.astype(jnp.float32))
```

```python
import jax
import jax.numpy as jnp
import numpy as np
from jax import lax
from jax.experimental import pallas as pl
from jax.experimental.pallas import tpu as pltpu
from jax.sharding import PartitionSpec as P

section_step = 0.1
NF, EA, EB, LEV = 4, 24, 8, 128
DEV, CAP, ROWS, WIDE = 128, 12, 16, 768
AUX, COLS, STATE = 1013, 768, 512
F32, BF16 = jnp.float32, jnp.bfloat16
VMEM = pltpu.VMEM


def node_tables():
    nodes = np.array([-1.0, -1.0 / np.sqrt(5.0), 1.0 / np.sqrt(5.0), 1.0])
    quadrature = np.array([1.0 / 6.0, 5.0 / 6.0, 5.0 / 6.0, 1.0 / 6.0])
    products = np.array(
        [np.prod([nodes[i] - nodes[k] for k in range(4) if k != i]) for i in range(4)]
    )
    derivative = np.zeros((4, 4))
    for i in range(4):
        for k in range(4):
            if i != k:
                derivative[i, k] = products[i] / (products[k] * (nodes[i] - nodes[k]))
            else:
                derivative[i, i] = sum(1.0 / (nodes[i] - nodes[m]) for m in range(4) if m != i)
    return derivative.astype(np.float32), quadrature.astype(np.float32)


def section_tables():
    d, w = node_tables()
    s = np.arange(8)
    up, j = s // 4, s % 4
    rows = []
    for p in range(2):
        i = 2 * p + up
        rows += [-d[i, up], -d[i, 1 - up], -d[i, 2 + up], -d[i, 3 - up]]
    rows += [-d[j, (j - shift) % 4] for shift in range(4)]
    rows += [w[2 * p + up] * w[j] for p in range(2)]
    return np.broadcast_to(np.stack(rows)[:, :, None], (14, 8, 128)).astype(np.float32).copy()


def sublane(shape):
    return lax.broadcasted_iota(jnp.int32, shape, len(shape) - 2)


def turn(x, shift):
    return pltpu.roll(x, shift % 8, axis=x.ndim - 2)


def pack_kernel(aux_ref, out_ref):
    row = lax.broadcasted_iota(jnp.int32, (512, 384), 0)
    lane = lax.broadcasted_iota(jnp.int32, (512, 384), 1)
    base, slot = row // ROWS * CAP, row % ROWS
    first = jnp.where((slot < CAP) & (lane == base + slot), 1.0, 0.0).astype(BF16)
    tail = aux_ref[WIDE:, :].astype(F32)
    tail = jnp.where(lax.broadcasted_iota(jnp.int32, tail.shape, 0) < AUX - WIDE, tail, 0.0).astype(BF16)
    nt = (((1,), (1,)), ((), ()))
    for part in range(3):
        rest = jnp.where((slot >= CAP) & (lane == base + slot - CAP + 4 * part), 1.0, 0.0).astype(BF16)
        piece = slice(256 * part, 256 * part + 256)
        out_ref[:, piece] = (
            lax.dot_general(first, aux_ref[piece, :], nt, preferred_element_type=F32)
            + lax.dot_general(rest, tail, nt, preferred_element_type=F32)
        ).astype(BF16)


def pack(aux_t):
    return pl.pallas_call(
        pack_kernel,
        grid=(4,),
        in_specs=[pl.BlockSpec((1024, 384), lambda g: (0, g))],
        out_specs=pl.BlockSpec((512, WIDE), lambda g: (g, 0)),
        out_shape=jax.ShapeDtypeStruct((DEV * ROWS, WIDE), BF16),
        compiler_params=pltpu.CompilerParams(vmem_limit_bytes=24 << 20),
        cost_estimate=pl.CostEstimate(flops=3_000_000_000, bytes_accessed=6_500_000, transcendentals=0),
    )(aux_t)


def section_kernel(tab_ref, prog_ref, mass_ref, sum_ref, edge_ref, state_ref, cells, sides):
    sub = sublane((EB, 8, LEV))
    j = sub % 4
    low = sub < 4
    is0, is3 = j == 0, j == 3

    def spread_row(a, _):
        tab = [tab_ref[k] for k in range(14)]
        weight = [tab[12 + p] * mass_ref[a, :, p] for p in range(2)]
        msum = []
        for p in range(2):
            t = weight[p] + turn(weight[p], 4)
            msum.append(1.0 / (t + turn(t, 7)))
        flow = [[weight[p] * prog_ref[f, a, :, p] for p in range(2)] for f in range(2)]
        for f in range(NF + 1):
            if f < NF:
                x = [prog_ref[f, a, :, p] for p in range(2)]
                xs = [turn(x[p], 4) for p in range(2)]
                value = []
                for p in range(2):
                    da = (
                        tab[4 * p] * x[0] + tab[4 * p + 1] * xs[0]
                        + tab[4 * p + 2] * x[1] + tab[4 * p + 3] * xs[1]
                    )
                    db = tab[8] * x[p]
                    for shift in range(1, 4):
                        moved = turn(x[p], shift)
                        moved = jnp.where(j >= shift, moved, turn(moved, 4))
                        db += tab[8 + shift] * moved
                    value.append(flow[0][p] * da + flow[1][p] * db)
                    t = weight[p] * x[p]
                    t = t + turn(t, 4)
                    t = (t + turn(t, 7)) * msum[p]
                    for b in range(EB):
                        for q in range(2):
                            cells[f, pl.ds(a * 32 + b * 4 + p * 2 + q, 1), :] = t[b, 2 * q : 2 * q + 1]
            else:
                value = weight
            for p in range(2):
                v = value[p]
                for up in range(2):
                    place = pl.ds(a * 4 + 2 * p + up, 1)
                    sides[0, f, place, :] = v[0, 4 * up : 4 * up + 1]
                    sides[1, f, place, :] = v[EB - 1, 4 * up + 3 : 4 * up + 4]
                after = jnp.concatenate([turn(v[:1] * 0.0, 0), turn(v[:-1], 5)], axis=0)
                before = jnp.concatenate([turn(v[1:], 3), v[:1] * 0.0], axis=0)
                sum_ref[f, a, :, p] = v + jnp.where(is0, after, jnp.where(is3, before, 0.0))
        return 0

    lax.fori_loop(0, EA, spread_row, 0)

    def join_rows(a, _):
        for f in range(NF + 1):
            here, there = sum_ref[f, a, :, 1], sum_ref[f, a + 1, :, 0]
            sum_ref[f, a, :, 1] = here + jnp.where(low, 0.0, turn(there, 4))
            sum_ref[f, a + 1, :, 0] = there + jnp.where(low, turn(here, 4), 0.0)
        return 0

    lax.fori_loop(0, EA - 1, join_rows, 0)
    row = lax.broadcasted_iota(jnp.int32, (EA * 4, LEV), 0)
    above, below = (row % 4 == 3) & (row < EA * 4 - 1), (row % 4 == 0) & (row > 0)
    for k in range(2):
        for f in range(NF + 1):
            v = sides[k, f]
            other = jnp.where(above, pltpu.roll(v, EA * 4 - 1, axis=0), jnp.where(below, pltpu.roll(v, 1, axis=0), 0.0))
            edge_ref[k, f] = (v + other).astype(BF16)
    for f in range(NF):
        state_ref[:, f * LEV : (f + 1) * LEV] = cells[f].astype(BF16)


def section(tab, prog, mass):
    return pl.pallas_call(
        section_kernel,
        in_specs=[pl.BlockSpec(memory_space=VMEM)] * 3,
        out_specs=[pl.BlockSpec(memory_space=VMEM)] * 3,
        out_shape=[
            jax.ShapeDtypeStruct((NF + 1, EA, EB, 2, 8, LEV), F32),
            jax.ShapeDtypeStruct((2, NF + 1, EA * 4, LEV), BF16),
            jax.ShapeDtypeStruct((COLS, STATE), BF16),
        ],
        scratch_shapes=[VMEM((NF, COLS, LEV), F32), VMEM((2, NF + 1, EA * 4, LEV), F32)],
        compiler_params=pltpu.CompilerParams(vmem_limit_bytes=40 << 20),
        cost_estimate=pl.CostEstimate(flops=20_000_000_000, bytes_accessed=16_000_000, transcendentals=0),
    )(tab, prog, mass)


def side_terms(sides, f, a, p):
    sub = sublane((8, LEV))
    low, j = sub < 4, sub % 4
    rows = [
        jnp.where(low, sides[k, f, pl.ds(a * 4 + 2 * p, 1), :], sides[k, f, pl.ds(a * 4 + 2 * p + 1, 1), :])
        for k in range(2)
    ]
    return jnp.where(j == 0, rows[0], 0.0), jnp.where(j == 3, rows[1], 0.0)


def rim_kernel(first_ref, last_ref, halo_ref, out_ref, sides):
    sides[...] = halo_ref[...].astype(F32)
    low = sublane((4, 8, LEV)) < 4
    for k, (ref, a, p) in enumerate(((first_ref, 0, 0), (last_ref, EA - 1, 1))):
        for f in range(NF + 1):
            left, right = side_terms(sides, f, a, p)
            rows = [ref[f, 0, b, 0] for b in range(EB)]
            rows[0] += left
            rows[-1] += right
            if p:
                rows = [turn(r, 4) for r in rows]
            packed = [jnp.where(low[0], rows[b], turn(rows[b + 1], 4)) for b in range(0, EB, 2)]
            out_ref[k, f * 32 : (f + 1) * 32] = jnp.concatenate(packed, axis=0).astype(BF16)


def rims(sums, halo):
    return pl.pallas_call(
        rim_kernel,
        grid=(1,),
        in_specs=[
            pl.BlockSpec((NF + 1, 1, EB, 1, 8, LEV), lambda g: (0, 0, 0, 0, 0, 0)),
            pl.BlockSpec((NF + 1, 1, EB, 1, 8, LEV), lambda g: (0, EA - 1, 0, 1, 0, 0)),
            pl.BlockSpec(halo.shape, lambda g: (0, 0, 0, 0)),
        ],
        out_specs=pl.BlockSpec((2, (NF + 1) * 32, LEV), lambda g: (0, 0, 0)),
        out_shape=jax.ShapeDtypeStruct((2, (NF + 1) * 32, LEV), BF16),
        scratch_shapes=[VMEM((2, NF + 1, EA * 4, LEV), F32)],
        compiler_params=pltpu.CompilerParams(vmem_limit_bytes=8 << 20),
    )(sums, sums, halo)


def close_kernel(sum_ref, prog_ref, halo_ref, rim_ref, out_ref, sides):
    sides[...] = halo_ref[...].astype(F32)
    low = sublane((8, LEV)) < 4

    def rim_terms(k, f):
        keep = low if k == 0 else jnp.logical_not(low)
        terms = []
        for pair in range(EB // 2):
            row = f * 32 + pair * 8
            both = rim_ref[k, row : row + 8].astype(F32)
            pieces = (both, turn(both, 4)) if k == 0 else (turn(both, 4), both)
            terms += [jnp.where(keep, piece, 0.0)[None] for piece in pieces]
        return jnp.concatenate(terms, axis=0)

    def close_half(a, p, rim):
        total = []
        for f in range(NF + 1):
            left, right = side_terms(sides, f, a, p)
            v = sum_ref[f, a, :, p]
            if rim is not None:
                v = v + rim_terms(rim, f)
            total.append(jnp.concatenate([v[:1] + left[None], v[1:-1], v[-1:] + right[None]], axis=0))
        scale = section_step / total[NF]
        for f in range(NF):
            out_ref[f, a, :, p] = prog_ref[f, a, :, p] + total[f] * scale

    def close_row(a, _):
        close_half(a, 0, None)
        close_half(a, 1, None)
        return 0

    close_half(0, 0, 0)
    close_half(0, 1, None)
    lax.fori_loop(1, EA - 1, close_row, 0)
    close_half(EA - 1, 0, None)
    close_half(EA - 1, 1, 1)


def close(sums, prog, halo, rim):
    return pl.pallas_call(
        close_kernel,
        in_specs=[pl.BlockSpec(memory_space=VMEM)] * 4,
        out_specs=pl.BlockSpec(memory_space=VMEM),
        out_shape=jax.ShapeDtypeStruct((NF, EA, EB, 2, 8, LEV), F32),
        scratch_shapes=[VMEM((2, NF + 1, EA * 4, LEV), F32)],
        compiler_params=pltpu.CompilerParams(vmem_limit_bytes=40 << 20),
        cost_estimate=pl.CostEstimate(flops=8_000_000_000, bytes_accessed=20_000_000, transcendentals=0),
    )(sums, prog, halo, rim)


def places_kernel(owner_ref, out_ref):
    owner = owner_ref[...]
    hit = sublane((DEV, COLS)) == owner
    hits = jnp.where(hit, 1.0, 0.0)
    lane = lax.broadcasted_iota(jnp.int32, (COLS, COLS), 1)
    before = jnp.where(sublane((COLS, COLS)) < lane, 1.0, 0.0).astype(BF16)
    earlier = jnp.dot(hits.astype(BF16), before, preferred_element_type=F32)
    slot = jnp.sum(hits * earlier, axis=0, keepdims=True).astype(jnp.int32)
    base = owner * ROWS
    none = jnp.full((1, COLS), -1, jnp.int32)
    rows = [base + slot]
    for part in range(3):
        rows.append(jnp.where(slot // 4 == part, base + CAP + slot - 4 * part, none))
    out_ref[...] = jnp.concatenate(rows + [none] * 4, axis=0)


def places(owner):
    return pl.pallas_call(
        places_kernel,
        in_specs=[pl.BlockSpec(memory_space=VMEM)],
        out_specs=pl.BlockSpec(memory_space=VMEM),
        out_shape=jax.ShapeDtypeStruct((8, COLS), jnp.int32),
        compiler_params=pltpu.CompilerParams(vmem_limit_bytes=16 << 20),
    )(owner)


def early_kernel(state_ref, win_ref, bias_ref, out_ref):
    out_ref[...] = jnp.dot(state_ref[...], win_ref[...], preferred_element_type=F32) + bias_ref[...]


def early(state, weight_in, bias_in):
    hid = weight_in.shape[1]
    return pl.pallas_call(
        early_kernel,
        grid=(4,),
        in_specs=[
            pl.BlockSpec((COLS, STATE), lambda g: (0, 0)),
            pl.BlockSpec((STATE, hid // 4), lambda g: (0, g)),
            pl.BlockSpec((1, hid // 4), lambda g: (0, g)),
        ],
        out_specs=pl.BlockSpec((COLS, hid // 4), lambda g: (0, g)),
        out_shape=jax.ShapeDtypeStruct((COLS, hid), F32),
        compiler_params=pltpu.CompilerParams(vmem_limit_bytes=24 << 20),
        cost_estimate=pl.CostEstimate(flops=2_000_000_000, bytes_accessed=10_000_000, transcendentals=0),
    )(state, weight_in, bias_in)


def tail_kernel(place_ref, home_ref, early_ref, win_ref, wout_ref, bout_ref, sec_ref, out_ref, inc):
    count = place_ref.shape[0]
    lane = lax.broadcasted_iota(jnp.int32, (count, DEV * ROWS), 1)

    def pick(k):
        return jnp.where(lane == place_ref[:, k : k + 1], 1.0, 0.0).astype(BF16)

    main = jnp.dot(pick(0), home_ref[...], preferred_element_type=F32).astype(BF16)
    rest = jnp.zeros((count, 256), F32)
    for part in range(3):
        rest += jnp.dot(pick(1 + part), home_ref[:, 256 * part : 256 * part + 256], preferred_element_type=F32)
    aux = jnp.concatenate([main, rest.astype(BF16)], axis=1)[:, :AUX]
    for half in range(2):
        cols = slice(1024 * half, 1024 * half + 1024)
        h = early_ref[:, cols] + jnp.dot(aux, win_ref[STATE:, cols], preferred_element_type=F32)
        h = (h / (1.0 + jnp.exp(-h))).astype(BF16)
        part = jnp.dot(h, wout_ref[cols, :], preferred_element_type=F32)
        total = part + bout_ref[...] if half == 0 else total + part
    total = total.astype(BF16).astype(F32)
    for f in range(NF):
        inc[f] = total[:, f * LEV : (f + 1) * LEV]
    rows_a = count // 32
    sub = sublane((8, LEV))
    right = sub % 4 >= 2
    for f in range(NF):

        def add(n, _):
            a, b = n // EB, n % EB
            for p in range(2):
                row = n * 4 + 2 * p
                term = jnp.where(right, inc[f, pl.ds(row + 1, 1), :], inc[f, pl.ds(row, 1), :])
                out_ref[f, a, b, p] = sec_ref[f, a, b, p] + term
            return 0

        lax.fori_loop(0, rows_a * EB, add, 0, unroll=8)


def tail(place, home, first, weight_in, weight_out, bias_out, sec):
    steps = 3
    count, rows_a = COLS // steps, EA // steps
    whole = pl.BlockSpec(memory_space=VMEM)
    block = pl.BlockSpec((NF, rows_a, EB, 2, 8, LEV), lambda g: (0, g, 0, 0, 0, 0))
    return pl.pallas_call(
        tail_kernel,
        grid=(steps,),
        in_specs=[
            pl.BlockSpec((count, 8), lambda g: (g, 0)),
            whole,
            pl.BlockSpec((count, first.shape[1]), lambda g: (g, 0)),
            whole,
            whole,
            whole,
            block,
        ],
        out_specs=block,
        out_shape=jax.ShapeDtypeStruct(sec.shape, F32),
        scratch_shapes=[VMEM((NF, count, LEV), F32)],
        compiler_params=pltpu.CompilerParams(vmem_limit_bytes=48 << 20),
        cost_estimate=pl.CostEstimate(flops=10_000_000_000, bytes_accessed=30_000_000, transcendentals=0),
    )(place, home, first, weight_in, weight_out, bias_out, sec)


def both_ways(pair, axis):
    count = lax.axis_size(axis)
    up = [(i, (i + 1) % count) for i in range(count)]
    down = [((i + 1) % count, i) for i in range(count)]
    return jnp.stack([lax.ppermute(pair[1], axis, up), lax.ppermute(pair[0], axis, down)])


def shards(prognostic, layer_mass, column_aux, group_owner, weight_in, bias_in, weight_out, bias_out):
    prog = prognostic.reshape(NF, EA, EB, 2, 8, LEV)
    mass = layer_mass.reshape(EA, EB, 2, 8, LEV)
    packed = pack(column_aux.T).reshape(DEV, ROWS, WIDE)
    home = lax.all_to_all(packed, ("curve", "sub"), split_axis=0, concat_axis=0, tiled=True)
    sums, edges, state = section(jnp.asarray(section_tables()), prog, mass)
    halo = both_ways(edges, "sub")
    place = places(group_owner.reshape(1, COLS)).T
    first = early(state, weight_in, bias_in[None])
    rim = both_ways(rims(sums, halo), "curve")
    sec = close(sums, prog, halo, rim)
    out = tail(place, home.reshape(DEV * ROWS, WIDE), first, weight_in, weight_out, bias_out[None], sec)
    return out.reshape(prognostic.shape)


def solution(mesh):
    return jax.shard_map(
        shards,
        mesh=mesh,
        in_specs=(
            P(None, "curve", "sub", None, None, None),
            P("curve", "sub", None, None, None),
            P(("curve", "sub"), None),
            P(("curve", "sub"), None),
            P(),
            P(),
            P(),
            P(),
        ),
        out_specs=P(None, "curve", "sub", None, None, None),
        check_vma=False,
    )
```

```python
import jax
import jax.numpy as jnp
import numpy as np
from jax import lax
from jax.experimental import pallas as pl
from jax.experimental.pallas import tpu as pltpu
from jax.sharding import PartitionSpec as P

section_step = 0.1
NF, EA, EB, LEV = 4, 24, 8, 128
DEV, CAP, ROWS, WIDE = 128, 12, 16, 768
AUX, COLS, STATE = 1013, 768, 512
F32, BF16 = jnp.float32, jnp.bfloat16
VMEM = pltpu.VMEM
GROUPS, GROUP = 4, 32
TURN = 53
TURN_BACK = pow(TURN, -1, DEV)


def node_tables():
    nodes = np.array([-1.0, -1.0 / np.sqrt(5.0), 1.0 / np.sqrt(5.0), 1.0])
    quadrature = np.array([1.0 / 6.0, 5.0 / 6.0, 5.0 / 6.0, 1.0 / 6.0])
    products = np.array(
        [np.prod([nodes[i] - nodes[k] for k in range(4) if k != i]) for i in range(4)]
    )
    derivative = np.zeros((4, 4))
    for i in range(4):
        for k in range(4):
            if i != k:
                derivative[i, k] = products[i] / (products[k] * (nodes[i] - nodes[k]))
            else:
                derivative[i, i] = sum(1.0 / (nodes[i] - nodes[m]) for m in range(4) if m != i)
    return derivative.astype(np.float32), quadrature.astype(np.float32)


def section_tables():
    d, w = node_tables()
    s = np.arange(8)
    up, j = s // 4, s % 4
    rows = []
    for p in range(2):
        i = 2 * p + up
        rows += [-d[i, up], -d[i, 1 - up], -d[i, 2 + up], -d[i, 3 - up]]
    rows += [-d[j, (j - shift) % 4] for shift in range(4)]
    rows += [w[2 * p + up] * w[j] for p in range(2)]
    return np.broadcast_to(np.stack(rows)[:, :, None], (14, 8, 128)).astype(np.float32).copy()


def sublane(shape):
    return lax.broadcasted_iota(jnp.int32, shape, len(shape) - 2)


def turn(x, shift):
    return pltpu.roll(x, shift % 8, axis=x.ndim - 2)


def pack_kernel(aux_ref, out_ref):
    row = lax.broadcasted_iota(jnp.int32, (512, 384), 0)
    lane = lax.broadcasted_iota(jnp.int32, (512, 384), 1)
    base, slot = row // ROWS * CAP, row % ROWS
    first = jnp.where((slot < CAP) & (lane == base + slot), 1.0, 0.0).astype(BF16)
    tail = aux_ref[WIDE:, :].astype(F32)
    tail = jnp.where(lax.broadcasted_iota(jnp.int32, tail.shape, 0) < AUX - WIDE, tail, 0.0).astype(BF16)
    nt = (((1,), (1,)), ((), ()))
    for part in range(3):
        rest = jnp.where((slot >= CAP) & (lane == base + slot - CAP + 4 * part), 1.0, 0.0).astype(BF16)
        piece = slice(256 * part, 256 * part + 256)
        out_ref[:, piece] = (
            lax.dot_general(first, aux_ref[piece, :], nt, preferred_element_type=F32)
            + lax.dot_general(rest, tail, nt, preferred_element_type=F32)
        ).astype(BF16)


def pack(aux_t):
    return pl.pallas_call(
        pack_kernel,
        grid=(4,),
        in_specs=[pl.BlockSpec((1024, 384), lambda g: (0, g))],
        out_specs=pl.BlockSpec((512, WIDE), lambda g: (g, 0)),
        out_shape=jax.ShapeDtypeStruct((DEV * ROWS, WIDE), BF16),
        compiler_params=pltpu.CompilerParams(vmem_limit_bytes=24 << 20),
        cost_estimate=pl.CostEstimate(flops=3_000_000_000, bytes_accessed=6_500_000, transcendentals=0),
    )(aux_t)


def section_rows(tab_ref, sec, mass, sums, sides, cells):
    sub = sublane((EB, 8, LEV))
    j = sub % 4
    low = sub < 4
    is0, is3 = j == 0, j == 3

    def spread_row(a, _):
        tab = [tab_ref[k] for k in range(14)]
        weight = [tab[12 + p] * mass[a, :, p] for p in range(2)]
        msum = []
        for p in range(2):
            t = weight[p] + turn(weight[p], 4)
            msum.append(1.0 / (t + turn(t, 7)))
        flow = [[weight[p] * sec[f, a, :, p] for p in range(2)] for f in range(2)]
        for f in range(NF + 1):
            if f < NF:
                x = [sec[f, a, :, p] for p in range(2)]
                xs = [turn(x[p], 4) for p in range(2)]
                value = []
                for p in range(2):
                    da = (
                        tab[4 * p] * x[0] + tab[4 * p + 1] * xs[0]
                        + tab[4 * p + 2] * x[1] + tab[4 * p + 3] * xs[1]
                    )
                    db = tab[8] * x[p]
                    for shift in range(1, 4):
                        moved = turn(x[p], shift)
                        moved = jnp.where(j >= shift, moved, turn(moved, 4))
                        db += tab[8 + shift] * moved
                    value.append(flow[0][p] * da + flow[1][p] * db)
                    t = weight[p] * x[p]
                    t = t + turn(t, 4)
                    t = (t + turn(t, 7)) * msum[p]
                    for b in range(EB):
                        for q in range(2):
                            cells[f, pl.ds(a * 32 + b * 4 + p * 2 + q, 1), :] = t[b, 2 * q : 2 * q + 1]
            else:
                value = weight
            for p in range(2):
                v = value[p]
                for up in range(2):
                    place = pl.ds(a * 4 + 2 * p + up, 1)
                    sides[0, f, place, :] = v[0, 4 * up : 4 * up + 1]
                    sides[1, f, place, :] = v[EB - 1, 4 * up + 3 : 4 * up + 4]
                none = jnp.zeros((1, 8, LEV), F32)
                after = jnp.concatenate([none, turn(v[:-1], 5)], axis=0)
                before = jnp.concatenate([turn(v[1:], 3), none], axis=0)
                sums[f, a, :, p] = v + jnp.where(is0, after, jnp.where(is3, before, 0.0))
        return 0

    lax.fori_loop(0, EA, spread_row, 0)

    def join_rows(a, _):
        for f in range(NF + 1):
            here, there = sums[f, a, :, 1], sums[f, a + 1, :, 0]
            sums[f, a, :, 1] = here + jnp.where(low, 0.0, turn(there, 4))
            sums[f, a + 1, :, 0] = there + jnp.where(low, turn(here, 4), 0.0)
        return 0

    lax.fori_loop(0, EA - 1, join_rows, 0)


def side_edges(sides, edge):
    row = lax.broadcasted_iota(jnp.int32, (EA * 4, LEV), 0)
    above, below = (row % 4 == 3) & (row < EA * 4 - 1), (row % 4 == 0) & (row > 0)
    for k in range(2):
        for f in range(NF + 1):
            v = sides[k, f]
            up, down = pltpu.roll(v, EA * 4 - 1, axis=0), pltpu.roll(v, 1, axis=0)
            edge[k, f] = (v + jnp.where(above, up, jnp.where(below, down, 0.0))).astype(BF16)


def side_terms(sides, f, a, p):
    sub = sublane((8, LEV))
    low, j = sub < 4, sub % 4
    rows = [
        jnp.where(low, sides[k, f, pl.ds(a * 4 + 2 * p, 1), :], sides[k, f, pl.ds(a * 4 + 2 * p + 1, 1), :])
        for k in range(2)
    ]
    return jnp.where(j == 0, rows[0], 0.0), jnp.where(j == 3, rows[1], 0.0)


def rim_rows(sums, sides, rim):
    low = sublane((8, LEV)) < 4
    for k, (a, p) in enumerate(((0, 0), (EA - 1, 1))):
        for f in range(NF + 1):
            left, right = side_terms(sides, f, a, p)
            rows = [sums[f, a, b, p] for b in range(EB)]
            rows[0] += left
            rows[-1] += right
            if p:
                rows = [turn(r, 4) for r in rows]
            packed = [jnp.where(low, rows[b], turn(rows[b + 1], 4)) for b in range(0, EB, 2)]
            rim[k, f * 32 : (f + 1) * 32] = jnp.concatenate(packed, axis=0).astype(BF16)


def close_rows(sums, sides, rim, sec):
    low = sublane((8, LEV)) < 4

    def rim_terms(k, f):
        keep = low if k == 0 else jnp.logical_not(low)
        terms = []
        for pair in range(EB // 2):
            row = f * 32 + pair * 8
            both = rim[k, row : row + 8].astype(F32)
            pieces = (both, turn(both, 4)) if k == 0 else (turn(both, 4), both)
            terms += [jnp.where(keep, piece, 0.0)[None] for piece in pieces]
        return jnp.concatenate(terms, axis=0)

    for k, (a, p) in enumerate(((0, 0), (EA - 1, 1))):
        for f in range(NF + 1):
            sums[f, a, :, p] += rim_terms(k, f)

    def close_row(a, _):
        for p in range(2):
            total = []
            for f in range(NF + 1):
                left, right = side_terms(sides, f, a, p)
                v = sums[f, a, :, p]
                total.append(jnp.concatenate([v[:1] + left[None], v[1:-1], v[-1:] + right[None]], axis=0))
            scale = section_step / total[NF]
            for f in range(NF):
                sec[f, a, :, p] += total[f] * scale
        return 0

    lax.fori_loop(0, EA, close_row, 0)


def find_places(owner_ref, mine, out):
    curve, x = mine
    owner = owner_ref[...]
    there = owner // 4
    rel = (
        (x - owner % 4) % 4
        + (curve // 8 - there // 8) % 4 * 4
        + (curve // 2 - there // 2) % 4 * 16
        + (curve - there) % 2 * 64
    )
    order = rel * TURN_BACK % DEV
    hits = jnp.where(sublane((DEV, COLS)) == order, 1.0, 0.0)
    lane = lax.broadcasted_iota(jnp.int32, (COLS, COLS), 1)
    before = jnp.where(sublane((COLS, COLS)) < lane, 1.0, 0.0).astype(BF16)
    earlier = jnp.dot(hits.astype(BF16), before, preferred_element_type=F32)
    slot = jnp.sum(hits * earlier, axis=0, keepdims=True)
    base = order.astype(F32) * ROWS
    none = jnp.full((1, COLS), -1.0, F32)
    rows = [base + slot]
    for part in range(3):
        inside = (slot >= 4 * part) & (slot < 4 * part + 4)
        rows.append(jnp.where(inside, base + CAP + slot - 4 * part, none))
    out[...] = jnp.transpose(jnp.concatenate(rows + [none] * 4, axis=0)).astype(jnp.int32)


def exchange_kernel(
    tab_ref, send_ref, owner_ref, bias_ref, prog_ref, mass_ref, win_ref, sec_out, early_out, aux_out,
    sec, mass, sums, sides, cells, home, win, early, state, acc, places, edge, edge_in, rim, rim_in,
    load_sem, store_sem, self_sem, send_sem, recv_sem, edge_send, edge_recv, rim_send, rim_recv,
):
    curve, x = lax.axis_index("curve"), lax.axis_index("sub")
    y, z, core = curve // 8, curve // 2 % 4, curve % 2
    me = curve * 4 + x
    mesh = pl.DeviceIdType.MESH

    loads = [
        pltpu.make_async_copy(prog_ref, sec, load_sem.at[0]),
        pltpu.make_async_copy(mass_ref, mass, load_sem.at[1]),
        pltpu.make_async_copy(win_ref.at[pl.ds(0, STATE)], win, load_sem.at[2]),
    ]
    for load in loads:
        load.start()

    barrier = pltpu.get_barrier_semaphore()

    def greet(d, _):
        t = lax.rem(me + d, DEV)
        pl.semaphore_signal(barrier, inc=1, device_id={"curve": t // 4, "sub": lax.rem(t, 4)}, device_id_type=mesh)
        return 0

    lax.fori_loop(1, DEV, greet, 0)
    pl.semaphore_wait(barrier, DEV - 1)

    own = pltpu.make_async_copy(send_ref.at[me], home.at[0], self_sem)
    own.start()

    def send_group(g):
        def send(o, _):
            rel = lax.rem(o * TURN, DEV)
            to_x = lax.rem(x + rel % 4, 4)
            to_curve = (
                lax.rem(y + rel // 4 % 4, 4) * 8 + lax.rem(z + rel // 16 % 4, 4) * 2 + lax.rem(core + rel // 64, 2)
            )
            pltpu.make_async_remote_copy(
                send_ref.at[to_curve * 4 + to_x], home.at[o], send_sem.at[g], recv_sem.at[g],
                device_id={"curve": to_curve, "sub": to_x}, device_id_type=mesh,
            ).start()
            return 0

        lax.fori_loop(max(1, GROUP * g), GROUP * g + GROUP, send, 0)

    def group_copy(g):
        span = pl.ds(max(1, GROUP * g), GROUP - (g == 0))
        return pltpu.make_async_remote_copy(
            send_ref.at[span], home.at[span], send_sem.at[g], recv_sem.at[g],
            device_id={"curve": curve, "sub": x}, device_id_type=mesh,
        )

    def select_group(g):
        group_copy(g).wait_recv()
        if g == 0:
            own.wait()

        def chunk(m, _):
            rows = pl.ds(m * 256, 256)
            lane = lax.broadcasted_iota(jnp.int32, (256, GROUP * ROWS), 1) + GROUP * ROWS * g

            def pick(k):
                return jnp.where(lane == places[rows, k : k + 1], 1.0, 0.0).astype(BF16)

            def block(lanes):
                return home[GROUP * g : GROUP * (g + 1), :, lanes].reshape(GROUP * ROWS, -1)

            main = jnp.dot(pick(0), block(slice(0, WIDE)), preferred_element_type=F32)
            rest = jnp.dot(pick(1), block(slice(0, 256)), preferred_element_type=F32)
            for part in range(1, 3):
                rest += jnp.dot(
                    pick(1 + part), block(slice(256 * part, 256 * part + 256)), preferred_element_type=F32
                )
            if g:
                main, rest = main + acc[rows, :WIDE], rest + acc[rows, WIDE:]
            if g < GROUPS - 1:
                acc[rows, :WIDE], acc[rows, WIDE:] = main, rest
            else:
                aux_out[rows, :WIDE], aux_out[rows, WIDE:] = main.astype(BF16), rest.astype(BF16)
            return 0

        lax.fori_loop(0, COLS // 256, chunk, 0)

    def both_ways(src, dst, send, recv, axis, place, count):
        return [
            pltpu.make_async_remote_copy(
                src.at[k], dst.at[1 - k], send.at[k], recv.at[1 - k],
                device_id={axis: lax.rem(place + (1 if k else count - 1), count)}, device_id_type=mesh,
            )
            for k in range(2)
        ]

    def await_both(copies):
        for copy in copies:
            copy.wait_recv()

    send_group(0)
    send_group(1)
    loads[0].wait()
    loads[1].wait()
    section_rows(tab_ref, sec, mass, sums, sides, cells)
    side_edges(sides, edge)
    edge_copies = both_ways(edge, edge_in, edge_send, edge_recv, "sub", x, 4)
    for copy in edge_copies:
        copy.start()
    send_group(2)

    for f in range(NF):
        state[:, f * LEV : (f + 1) * LEV] = cells[f].astype(BF16)
    find_places(owner_ref, (curve, x), places)
    loads[2].wait()

    def early_tile(t, _):
        lanes = pl.ds(pl.multiple_of(t * 256, 256), 256)
        early[:, lanes] = jnp.dot(state[...], win[:, lanes], preferred_element_type=F32) + bias_ref[:, lanes]
        return 0

    lax.fori_loop(0, early.shape[1] // 256, early_tile, 0)
    early_store = pltpu.make_async_copy(early, early_out, store_sem.at[0])
    early_store.start()

    await_both(edge_copies)
    sides[...] = edge_in[...].astype(F32)
    rim_rows(sums, sides, rim)
    rim_copies = both_ways(rim, rim_in, rim_send, rim_recv, "curve", curve, 32)
    for copy in rim_copies:
        copy.start()
    send_group(3)

    select_group(0)
    select_group(1)
    await_both(rim_copies)
    close_rows(sums, sides, rim_in, sec)
    sec_store = pltpu.make_async_copy(sec, sec_out, store_sem.at[1])
    sec_store.start()
    select_group(2)
    select_group(3)
    for g in range(GROUPS):
        group_copy(g).wait_send()
    for copy in edge_copies + rim_copies:
        copy.wait_send()
    early_store.wait()
    sec_store.wait()


def exchange(tab, packed, owner, bias_in, prog, mass, weight_in):
    hid = weight_in.shape[1]
    vm, hbm = pl.BlockSpec(memory_space=VMEM), pl.BlockSpec(memory_space=pl.ANY)
    dma = pltpu.SemaphoreType.DMA
    return pl.pallas_call(
        exchange_kernel,
        in_specs=[vm, vm, vm, vm, hbm, hbm, hbm],
        out_specs=[hbm, hbm, vm],
        out_shape=[
            jax.ShapeDtypeStruct(prog.shape, F32),
            jax.ShapeDtypeStruct((COLS, hid), F32),
            jax.ShapeDtypeStruct((COLS, WIDE + 256), BF16),
        ],
        scratch_shapes=[
            VMEM(prog.shape, F32),
            VMEM(mass.shape, F32),
            VMEM((NF + 1, EA, EB, 2, 8, LEV), F32),
            VMEM((2, NF + 1, EA * 4, LEV), F32),
            VMEM((NF, COLS, LEV), F32),
            VMEM((DEV, ROWS, WIDE), BF16),
            VMEM((STATE, hid), BF16),
            VMEM((COLS, hid), F32),
            VMEM((COLS, STATE), BF16),
            VMEM((COLS, WIDE + 256), F32),
            VMEM((COLS, 8), jnp.int32),
            VMEM((2, NF + 1, EA * 4, LEV), BF16),
            VMEM((2, NF + 1, EA * 4, LEV), BF16),
            VMEM((2, (NF + 1) * 32, LEV), BF16),
            VMEM((2, (NF + 1) * 32, LEV), BF16),
            dma((3,)), dma((2,)), dma, dma((GROUPS,)), dma((GROUPS,)), dma((2,)), dma((2,)), dma((2,)), dma((2,)),
        ],
        compiler_params=pltpu.CompilerParams(
            collective_id=1, has_side_effects=True, vmem_limit_bytes=56 << 20
        ),
        cost_estimate=pl.CostEstimate(flops=10_000_000_000, bytes_accessed=40_000_000, transcendentals=0),
    )(tab, packed, owner, bias_in, prog, mass, weight_in)


def tail_kernel(
    aux_ref, early_ref, wa_ref, wb_ref, wout_ref, bout_ref, sec_ref, out_ref, sec, inc, total, load_sem, store_sem
):
    step = pl.program_id(0)
    rows_a = 4
    pieces = [pl.ds(n * rows_a, rows_a) for n in range(EA // rows_a)]

    @pl.when(step == 0)
    def _():
        pltpu.make_async_copy(sec_ref, sec, load_sem).start()

    h = (
        early_ref[...]
        + jnp.dot(aux_ref[:, :STATE], wa_ref[...], preferred_element_type=F32)
        + jnp.dot(aux_ref[:, STATE:AUX], wb_ref[: AUX - STATE, :], preferred_element_type=F32)
    )
    h = (h / (1.0 + jnp.exp(-h))).astype(BF16)
    part = jnp.dot(h, wout_ref[...], preferred_element_type=F32)

    @pl.when(step == 0)
    def _():
        total[...] = part + bout_ref[...]

    @pl.when(step > 0)
    def _():
        total[...] += part

    @pl.when(step == pl.num_programs(0) - 1)
    def _():
        pltpu.make_async_copy(sec_ref, sec, load_sem).wait()
        right = sublane((8, LEV)) % 4 >= 2
        stores = []
        for n, piece in enumerate(pieces):
            count = rows_a * 32
            for f in range(NF):
                inc[f] = total[n * count : (n + 1) * count, f * LEV : (f + 1) * LEV].astype(BF16).astype(F32)
                for e in range(rows_a * EB):
                    for p in range(2):
                        row = e * 4 + 2 * p
                        term = jnp.where(right, inc[f, row + 1 : row + 2, :], inc[f, row : row + 1, :])
                        sec[f, n * rows_a + e // EB, e % EB, p] += term
            store = pltpu.make_async_copy(sec.at[:, piece], out_ref.at[:, piece], store_sem.at[n])
            store.start()
            stores.append(store)
        for store in stores:
            store.wait()


def tail(aux, early, weight_in, weight_out, bias_out, sec):
    steps = 4
    hid = early.shape[1]
    tile = hid // steps
    hbm = pl.BlockSpec(memory_space=pl.ANY)
    return pl.pallas_call(
        tail_kernel,
        grid=(steps,),
        in_specs=[
            pl.BlockSpec(aux.shape, lambda t: (0, 0)),
            pl.BlockSpec((COLS, tile), lambda t: (0, t)),
            pl.BlockSpec((STATE, tile), lambda t: (1, t)),
            pl.BlockSpec((STATE, tile), lambda t: (2, t)),
            pl.BlockSpec((tile, STATE), lambda t: (t, 0)),
            pl.BlockSpec((1, STATE), lambda t: (0, 0)),
            hbm,
        ],
        out_specs=hbm,
        out_shape=jax.ShapeDtypeStruct(sec.shape, F32),
        scratch_shapes=[
            VMEM(sec.shape, F32),
            VMEM((NF, 128, LEV), F32),
            VMEM((COLS, STATE), F32),
            pltpu.SemaphoreType.DMA,
            pltpu.SemaphoreType.DMA((EA // 4,)),
        ],
        compiler_params=pltpu.CompilerParams(vmem_limit_bytes=40 << 20),
        cost_estimate=pl.CostEstimate(flops=5_000_000_000, bytes_accessed=30_000_000, transcendentals=0),
    )(aux, early, weight_in, weight_in, weight_out, bias_out, sec)


def shards(prognostic, layer_mass, column_aux, group_owner, weight_in, bias_in, weight_out, bias_out):
    prog = prognostic.reshape(NF, EA, EB, 2, 8, LEV)
    mass = layer_mass.reshape(EA, EB, 2, 8, LEV)
    packed = pack(column_aux.T).reshape(DEV, ROWS, WIDE)
    sec, early, aux = exchange(
        jnp.asarray(section_tables()), packed, group_owner.reshape(1, COLS), bias_in[None], prog, mass, weight_in
    )
    out = tail(aux, early, weight_in, weight_out, bias_out[None], sec)
    return out.reshape(prognostic.shape)


def solution(mesh):
    return jax.shard_map(
        shards,
        mesh=mesh,
        in_specs=(
            P(None, "curve", "sub", None, None, None),
            P("curve", "sub", None, None, None),
            P(("curve", "sub"), None),
            P(("curve", "sub"), None),
            P(),
            P(),
            P(),
            P(),
        ),
        out_specs=P(None, "curve", "sub", None, None, None),
        check_vma=False,
    )
```

```python
import jax
import jax.numpy as jnp
import numpy as np
from jax import lax
from jax.experimental import pallas as pl
from jax.experimental.pallas import tpu as pltpu
from jax.sharding import PartitionSpec as P

section_step = 0.1
NF, EA, EB, LEV = 4, 24, 8, 128
DEV, CAP, ROWS, WIDE = 128, 12, 16, 768
AUX, COLS, STATE = 1013, 768, 512
F32, BF16 = jnp.float32, jnp.bfloat16
VMEM = pltpu.VMEM
EXCHANGE_VMEM, TAIL_VMEM = 51, 44
BOUNDS = (0, 56, 88, 112, 128)
GROUPS = len(BOUNDS) - 1
TURN = 53
TURN_BACK = pow(TURN, -1, DEV)


def node_tables():
    nodes = np.array([-1.0, -1.0 / np.sqrt(5.0), 1.0 / np.sqrt(5.0), 1.0])
    quadrature = np.array([1.0 / 6.0, 5.0 / 6.0, 5.0 / 6.0, 1.0 / 6.0])
    products = np.array(
        [np.prod([nodes[i] - nodes[k] for k in range(4) if k != i]) for i in range(4)]
    )
    derivative = np.zeros((4, 4))
    for i in range(4):
        for k in range(4):
            if i != k:
                derivative[i, k] = products[i] / (products[k] * (nodes[i] - nodes[k]))
            else:
                derivative[i, i] = sum(1.0 / (nodes[i] - nodes[m]) for m in range(4) if m != i)
    return derivative.astype(np.float32), quadrature.astype(np.float32)


def section_tables():
    d, w = node_tables()
    s = np.arange(8)
    up, j = s // 4, s % 4
    rows = []
    for p in range(2):
        i = 2 * p + up
        rows += [-d[i, up], -d[i, 1 - up], -d[i, 2 + up], -d[i, 3 - up]]
    rows += [-d[j, (j - shift) % 4] for shift in range(4)]
    rows += [w[2 * p + up] * w[j] for p in range(2)]
    return [[float(v) for v in row] for row in rows]


def sublane(shape):
    return lax.broadcasted_iota(jnp.int32, shape, len(shape) - 2)


def turn(x, shift):
    return pltpu.roll(x, shift % 8, axis=x.ndim - 2)


def pack_tables(pick):
    row = lax.broadcasted_iota(jnp.int32, (512, 384), 0)
    lane = lax.broadcasted_iota(jnp.int32, (512, 384), 1)
    base, slot = row // ROWS * CAP, row % ROWS
    for part in range(3):
        pick[part, :, :384] = jnp.where((slot < CAP) & (lane == base + slot), 1.0, 0.0).astype(BF16)
        pick[part, :, 384:] = jnp.where((slot >= CAP) & (lane == base + slot - CAP + 4 * part), 1.0, 0.0).astype(BF16)


def pack_block(aux, pick, packed, block):
    lanes = slice(384 * block, 384 * block + 384)
    last = aux[WIDE:, lanes].astype(F32)
    last = jnp.concatenate([last, jnp.zeros((WIDE + 256 - AUX, 384), F32)], axis=0).astype(BF16)
    for part in range(3):
        piece = slice(256 * part, 256 * part + 256)
        value = lax.dot_general(
            pick[part], jnp.concatenate([aux[piece, lanes], last], axis=1), (((1,), (1,)), ((), ())),
            preferred_element_type=F32,
        )
        packed[32 * block : 32 * block + 32, :, piece] = value.astype(BF16).reshape(32, ROWS, 256)


def section_rows(tab_ref, sec, mass, sums, sides, cells):
    sub = sublane((EB, 8, LEV))
    j = sub % 4
    low = sub < 4
    is0, is3 = j == 0, j == 3

    def spread_row(a, _):
        tab = [tab_ref[k] for k in range(14)]
        weight = [tab[12 + p] * mass[a, :, p] for p in range(2)]
        msum = []
        for p in range(2):
            t = weight[p] + turn(weight[p], 4)
            msum.append(1.0 / (t + turn(t, 7)))
        flow = [[weight[p] * sec[f, a, :, p] for p in range(2)] for f in range(2)]
        for f in range(NF + 1):
            if f < NF:
                x = [sec[f, a, :, p] for p in range(2)]
                xs = [turn(x[p], 4) for p in range(2)]
                value = []
                for p in range(2):
                    da = (
                        tab[4 * p] * x[0] + tab[4 * p + 1] * xs[0]
                        + tab[4 * p + 2] * x[1] + tab[4 * p + 3] * xs[1]
                    )
                    db = tab[8] * x[p]
                    for shift in range(1, 4):
                        moved = turn(x[p], shift)
                        moved = jnp.where(j >= shift, moved, turn(moved, 4))
                        db += tab[8 + shift] * moved
                    value.append(flow[0][p] * da + flow[1][p] * db)
                    t = weight[p] * x[p]
                    t = t + turn(t, 4)
                    t = (t + turn(t, 7)) * msum[p]
                    for b in range(EB):
                        for q in range(2):
                            cells[f, pl.ds(a * 32 + b * 4 + p * 2 + q, 1), :] = t[b, 2 * q : 2 * q + 1]
            else:
                value = weight
            for p in range(2):
                v = value[p]
                for up in range(2):
                    place = pl.ds(a * 4 + 2 * p + up, 1)
                    sides[0, f, place, :] = v[0, 4 * up : 4 * up + 1]
                    sides[1, f, place, :] = v[EB - 1, 4 * up + 3 : 4 * up + 4]
                none = jnp.zeros((1, 8, LEV), F32)
                after = jnp.concatenate([none, turn(v[:-1], 5)], axis=0)
                before = jnp.concatenate([turn(v[1:], 3), none], axis=0)
                sums[f, a, :, p] = v + jnp.where(is0, after, jnp.where(is3, before, 0.0))
        return 0

    lax.fori_loop(0, EA, spread_row, 0)

    def join_rows(a, _):
        for f in range(NF + 1):
            here, there = sums[f, a, :, 1], sums[f, a + 1, :, 0]
            sums[f, a, :, 1] = here + jnp.where(low, 0.0, turn(there, 4))
            sums[f, a + 1, :, 0] = there + jnp.where(low, turn(here, 4), 0.0)
        return 0

    lax.fori_loop(0, EA - 1, join_rows, 0)


def side_edges(sides, edge):
    row = lax.broadcasted_iota(jnp.int32, (EA * 4, LEV), 0)
    above, below = (row % 4 == 3) & (row < EA * 4 - 1), (row % 4 == 0) & (row > 0)
    for k in range(2):
        for f in range(NF + 1):
            v = sides[k, f]
            up, down = pltpu.roll(v, EA * 4 - 1, axis=0), pltpu.roll(v, 1, axis=0)
            edge[k, f] = (v + jnp.where(above, up, jnp.where(below, down, 0.0))).astype(BF16)


def side_terms(sides, f, a, p):
    sub = sublane((8, LEV))
    low, j = sub < 4, sub % 4
    rows = [
        jnp.where(low, sides[k, f, pl.ds(a * 4 + 2 * p, 1), :], sides[k, f, pl.ds(a * 4 + 2 * p + 1, 1), :])
        for k in range(2)
    ]
    return jnp.where(j == 0, rows[0], 0.0), jnp.where(j == 3, rows[1], 0.0)


def rim_rows(sums, sides, rim):
    low = sublane((8, LEV)) < 4
    for k, (a, p) in enumerate(((0, 0), (EA - 1, 1))):
        for f in range(NF + 1):
            left, right = side_terms(sides, f, a, p)
            rows = [sums[f, a, b, p] for b in range(EB)]
            rows[0] += left
            rows[-1] += right
            if p:
                rows = [turn(r, 4) for r in rows]
            packed = [jnp.where(low, rows[b], turn(rows[b + 1], 4)) for b in range(0, EB, 2)]
            rim[k, f * 32 : (f + 1) * 32] = jnp.concatenate(packed, axis=0).astype(BF16)


def close_rows(sums, sides, rim, sec):
    low = sublane((8, LEV)) < 4

    def rim_terms(k, f):
        keep = low if k == 0 else jnp.logical_not(low)
        terms = []
        for pair in range(EB // 2):
            row = f * 32 + pair * 8
            both = rim[k, row : row + 8].astype(F32)
            pieces = (both, turn(both, 4)) if k == 0 else (turn(both, 4), both)
            terms += [jnp.where(keep, piece, 0.0)[None] for piece in pieces]
        return jnp.concatenate(terms, axis=0)

    for k, (a, p) in enumerate(((0, 0), (EA - 1, 1))):
        for f in range(NF + 1):
            sums[f, a, :, p] += rim_terms(k, f)

    def close_row(a, _):
        for p in range(2):
            total = []
            for f in range(NF + 1):
                left, right = side_terms(sides, f, a, p)
                v = sums[f, a, :, p]
                total.append(jnp.concatenate([v[:1] + left[None], v[1:-1], v[-1:] + right[None]], axis=0))
            scale = section_step / total[NF]
            for f in range(NF):
                sec[f, a, :, p] += total[f] * scale
        return 0

    lax.fori_loop(0, EA, close_row, 0)


def find_places(owner_ref, mine, out):
    curve, x = mine
    owner = owner_ref[...]
    there = owner // 4
    rel = (
        (x - owner % 4) % 4
        + (curve // 8 - there // 8) % 4 * 4
        + (curve // 2 - there // 2) % 4 * 16
        + (curve - there) % 2 * 64
    )
    order = rel * TURN_BACK % DEV
    hits = jnp.where(sublane((DEV, COLS)) == order, 1.0, 0.0)
    lane = lax.broadcasted_iota(jnp.int32, (COLS, COLS), 1)
    before = jnp.where(sublane((COLS, COLS)) < lane, 1.0, 0.0).astype(BF16)
    earlier = jnp.dot(hits.astype(BF16), before, preferred_element_type=F32)
    slot = jnp.sum(hits * earlier, axis=0, keepdims=True)
    base = order.astype(F32) * ROWS
    part = (slot >= 4).astype(F32) + (slot >= 8).astype(F32)
    rows = [base + slot, base + CAP + slot - 4 * part, part]
    out[...] = jnp.transpose(jnp.concatenate(rows + [part] * 5, axis=0)).astype(jnp.int32)


def exchange_kernel(
    owner_hbm, aux_ref, prog_ref, mass_ref, win_ref, sec_out, early_out, aux_out,
    tab_ref, owner_ref,
    aux, pick, packed, sec, mass, sums, sides, cells, home, win, early, state, acc, places, edge, edge_in, rim, rim_in,
    aux_sem, load_sem, store_sem, self_sem, send_sem, recv_sem, edge_send, edge_recv, rim_send, rim_recv,
):
    curve, x = lax.axis_index("curve"), lax.axis_index("sub")
    y, z, core = curve // 8, curve // 2 % 4, curve % 2
    me = curve * 4 + x
    mesh = pl.DeviceIdType.MESH

    loads = [
        pltpu.make_async_copy(prog_ref, sec, load_sem.at[0]),
        pltpu.make_async_copy(mass_ref, mass, load_sem.at[1]),
        pltpu.make_async_copy(win_ref.at[pl.ds(0, STATE)], win, load_sem.at[2]),
        pltpu.make_async_copy(owner_hbm, owner_ref, load_sem.at[3]),
    ]
    slots = [pl.ds(384 * n, 384) for n in range(4)]
    aux_loads = [pltpu.make_async_copy(aux_ref.at[:, s], aux.at[:, s], aux_sem.at[n]) for n, s in enumerate(slots)]
    for load in aux_loads + loads:
        load.start()

    barrier = pltpu.get_barrier_semaphore()

    def greet(d, _):
        t = lax.rem(me + d, DEV)
        pl.semaphore_signal(barrier, inc=1, device_id={"curve": t // 4, "sub": lax.rem(t, 4)}, device_id_type=mesh)
        return 0

    lax.fori_loop(1, DEV, greet, 0)
    pack_tables(pick)
    for n in range(4):
        aux_loads[n].wait()
        pack_block(aux, pick, packed, n)
    pl.semaphore_wait(barrier, DEV - 1)

    own = pltpu.make_async_copy(packed.at[me], home.at[0], self_sem)
    own.start()

    def send_group(g):
        def send(o, _):
            rel = lax.rem(o * TURN, DEV)
            to_x = lax.rem(x + rel % 4, 4)
            to_curve = (
                lax.rem(y + rel // 4 % 4, 4) * 8 + lax.rem(z + rel // 16 % 4, 4) * 2 + lax.rem(core + rel // 64, 2)
            )
            pltpu.make_async_remote_copy(
                packed.at[to_curve * 4 + to_x], home.at[o], send_sem.at[g], recv_sem.at[g],
                device_id={"curve": to_curve, "sub": to_x}, device_id_type=mesh,
            ).start()
            return 0

        lax.fori_loop(max(1, BOUNDS[g]), BOUNDS[g + 1], send, 0)

    def group_copy(g):
        first = max(1, BOUNDS[g])
        span = pl.ds(first, BOUNDS[g + 1] - first)
        return pltpu.make_async_remote_copy(
            packed.at[span], home.at[span], send_sem.at[g], recv_sem.at[g],
            device_id={"curve": curve, "sub": x}, device_id_type=mesh,
        )

    def select_group(g):
        group_copy(g).wait_recv()
        if g == 0:
            own.wait()

        depth = (BOUNDS[g + 1] - BOUNDS[g]) * ROWS

        def chunk(m, _):
            rows = pl.ds(m * 256, 256)
            lane = lax.broadcasted_iota(jnp.int32, (256, depth), 1) + BOUNDS[g] * ROWS

            def pick(k):
                return jnp.where(lane == places[rows, k : k + 1], 1.0, 0.0).astype(BF16)

            block = home[BOUNDS[g] : BOUNDS[g + 1]].reshape(depth, WIDE)
            main = jnp.dot(pick(0), block, preferred_element_type=F32)
            rest = jnp.dot(pick(1), block, preferred_element_type=F32)
            part = places[rows, 2:3]
            rest = jnp.where(part == 0, rest[:, :256], jnp.where(part == 1, rest[:, 256:512], rest[:, 512:]))
            if g:
                main, rest = main + acc[rows, :WIDE], rest + acc[rows, WIDE:]
            if g < GROUPS - 1:
                acc[rows, :WIDE], acc[rows, WIDE:] = main, rest
            else:
                aux_out[rows, :WIDE], aux_out[rows, WIDE:] = main.astype(BF16), rest.astype(BF16)
            return 0

        lax.fori_loop(0, COLS // 256, chunk, 0)

    def both_ways(src, dst, send, recv, axis, place, count):
        return [
            pltpu.make_async_remote_copy(
                src.at[k], dst.at[1 - k], send.at[k], recv.at[1 - k],
                device_id={axis: lax.rem(place + (1 if k else count - 1), count)}, device_id_type=mesh,
            )
            for k in range(2)
        ]

    def await_both(copies):
        for copy in copies:
            copy.wait_recv()

    send_group(0)
    loads[0].wait()
    loads[1].wait()
    sub = sublane((8, LEV))
    for k, row in enumerate(section_tables()):
        value = jnp.full((8, LEV), row[0], F32)
        for n in range(1, 8):
            value = jnp.where(sub == n, row[n], value)
        tab_ref[k] = value
    section_rows(tab_ref, sec, mass, sums, sides, cells)
    side_edges(sides, edge)
    edge_copies = both_ways(edge, edge_in, edge_send, edge_recv, "sub", x, 4)
    for copy in edge_copies:
        copy.start()
    send_group(1)

    for f in range(NF):
        state[:, f * LEV : (f + 1) * LEV] = cells[f].astype(BF16)
    loads[3].wait()
    find_places(owner_ref, (curve, x), places)
    loads[2].wait()

    def early_tile(t, _):
        lanes = pl.ds(pl.multiple_of(t * 256, 256), 256)
        early[:, lanes] = jnp.dot(state[...], win[:, lanes], preferred_element_type=F32)
        return 0

    lax.fori_loop(0, early.shape[1] // 256, early_tile, 0)
    early_store = pltpu.make_async_copy(early, early_out, store_sem.at[0])
    early_store.start()

    await_both(edge_copies)
    sides[...] = edge_in[...].astype(F32)
    rim_rows(sums, sides, rim)
    rim_copies = both_ways(rim, rim_in, rim_send, rim_recv, "curve", curve, 32)
    for copy in rim_copies:
        copy.start()
    send_group(2)
    send_group(3)

    select_group(0)
    select_group(1)
    await_both(rim_copies)
    close_rows(sums, sides, rim_in, sec)
    sec_store = pltpu.make_async_copy(sec, sec_out, store_sem.at[1])
    sec_store.start()
    select_group(2)
    select_group(3)
    for g in range(GROUPS):
        group_copy(g).wait_send()
    for copy in edge_copies + rim_copies:
        copy.wait_send()
    early_store.wait()
    sec_store.wait()


def exchange(owner, aux_t, prog, mass, weight_in):
    hid = weight_in.shape[1]
    vm, hbm = pl.BlockSpec(memory_space=VMEM), pl.BlockSpec(memory_space=pl.ANY)
    dma = pltpu.SemaphoreType.DMA
    return pl.pallas_call(
        exchange_kernel,
        in_specs=[hbm] * 5,
        out_specs=[hbm, hbm, vm],
        out_shape=[
            jax.ShapeDtypeStruct(prog.shape, F32),
            jax.ShapeDtypeStruct((COLS, hid), F32),
            jax.ShapeDtypeStruct((COLS, WIDE + 256), BF16),
        ],
        scratch_shapes=[
            VMEM((14, 8, LEV), F32),
            VMEM(owner.shape, jnp.int32),
            VMEM(aux_t.shape, BF16),
            VMEM((3, 512, WIDE), BF16),
            VMEM((DEV, ROWS, WIDE), BF16),
            VMEM(prog.shape, F32),
            VMEM(mass.shape, F32),
            VMEM((NF + 1, EA, EB, 2, 8, LEV), F32),
            VMEM((2, NF + 1, EA * 4, LEV), F32),
            VMEM((NF, COLS, LEV), F32),
            VMEM((DEV, ROWS, WIDE), BF16),
            VMEM((STATE, hid), BF16),
            VMEM((COLS, hid), F32),
            VMEM((COLS, STATE), BF16),
            VMEM((COLS, WIDE + 256), F32),
            VMEM((COLS, 8), jnp.int32),
            VMEM((2, NF + 1, EA * 4, LEV), BF16),
            VMEM((2, NF + 1, EA * 4, LEV), BF16),
            VMEM((2, (NF + 1) * 32, LEV), BF16),
            VMEM((2, (NF + 1) * 32, LEV), BF16),
            dma((4,)), dma((4,)), dma((2,)), dma, dma((GROUPS,)), dma((GROUPS,)), dma((2,)), dma((2,)), dma((2,)), dma((2,)),
        ],
        compiler_params=pltpu.CompilerParams(
            collective_id=1, has_side_effects=True, vmem_limit_bytes=EXCHANGE_VMEM << 20
        ),
        cost_estimate=pl.CostEstimate(flops=10_000_000_000, bytes_accessed=40_000_000, transcendentals=0),
    )(owner, aux_t, prog, mass, weight_in)


def tail_kernel(aux_ref, early_ref, win_ref, bin_ref, wout_ref, bout_ref, sec_ref, out_ref, inc, spread):
    step, last = pl.program_id(0), pl.num_programs(0) - 1
    count = aux_ref.shape[0]

    def add_block():
        term = jnp.dot(spread[...], inc[...], preferred_element_type=F32)
        for f in range(NF):
            piece = term[:, f * LEV : (f + 1) * LEV].reshape(sec_ref.shape[1:])
            out_ref[f] = sec_ref[f] + piece

    def network_block():
        total = bout_ref[...]
        aux = aux_ref[:, :AUX]
        for n in range(2):
            lanes = slice(1024 * n, 1024 * n + 1024)
            h = early_ref[:, lanes] + bin_ref[:, lanes] + jnp.dot(aux, win_ref[STATE:, lanes], preferred_element_type=F32)
            h = (h / (1.0 + jnp.exp(-h))).astype(BF16)
            total = total + jnp.dot(h, wout_ref[lanes, :], preferred_element_type=F32)
        return total.astype(BF16)

    def keep(total):
        inc[...] = total

    @pl.when(step == 0)
    def _():
        row = lax.broadcasted_iota(jnp.int32, spread.shape, 0)
        cell = row // 16 * 4 + row // 8 % 2 * 2 + row % 4 // 2
        lane = lax.broadcasted_iota(jnp.int32, spread.shape, 1)
        spread[...] = jnp.where(lane == cell, 1.0, 0.0).astype(BF16)
        keep(network_block())

    @pl.when((step > 0) & (step < last))
    def _():
        add_block()
        keep(network_block())

    @pl.when(step == last)
    def _():
        add_block()


def tail(aux, early, weight_in, bias_in, weight_out, bias_out, sec):
    steps = 3
    count, rows_a = COLS // steps, EA // steps
    ahead, behind = lambda n: jnp.minimum(n, steps - 1), lambda n: jnp.maximum(n - 1, 0)
    whole = pl.BlockSpec(memory_space=VMEM)
    block = pl.BlockSpec((NF, rows_a, EB, 2, 8, LEV), lambda n: (0, behind(n), 0, 0, 0, 0))
    return pl.pallas_call(
        tail_kernel,
        grid=(steps + 1,),
        in_specs=[
            pl.BlockSpec((count, aux.shape[1]), lambda n: (ahead(n), 0)),
            pl.BlockSpec((count, early.shape[1]), lambda n: (ahead(n), 0)),
            whole,
            whole,
            whole,
            whole,
            block,
        ],
        out_specs=block,
        out_shape=jax.ShapeDtypeStruct(sec.shape, F32),
        scratch_shapes=[VMEM((count, STATE), BF16), VMEM((4 * count, count), BF16)],
        compiler_params=pltpu.CompilerParams(vmem_limit_bytes=TAIL_VMEM << 20),
        cost_estimate=pl.CostEstimate(flops=5_000_000_000, bytes_accessed=30_000_000, transcendentals=0),
    )(aux, early, weight_in, bias_in, weight_out, bias_out, sec)


def shards(prognostic, layer_mass, column_aux, group_owner, weight_in, bias_in, weight_out, bias_out):
    prog = prognostic.reshape(NF, EA, EB, 2, 8, LEV)
    mass = layer_mass.reshape(EA, EB, 2, 8, LEV)
    sec, early, aux = exchange(
        group_owner.reshape(1, COLS), column_aux.T, prog, mass, weight_in
    )
    out = tail(aux, early, weight_in, bias_in[None], weight_out, bias_out[None], sec)
    return out.reshape(prognostic.shape)


def solution(mesh):
    return jax.shard_map(
        shards,
        mesh=mesh,
        in_specs=(
            P(None, "curve", "sub", None, None, None),
            P("curve", "sub", None, None, None),
            P(("curve", "sub"), None),
            P(("curve", "sub"), None),
            P(),
            P(),
            P(),
            P(),
        ),
        out_specs=P(None, "curve", "sub", None, None, None),
        check_vma=False,
    )
```

```python
import jax
import jax.numpy as jnp
import numpy as np
from jax import lax
from jax.experimental import pallas as pl
from jax.experimental.pallas import tpu as pltpu
from jax.sharding import PartitionSpec as P

section_step = 0.1
NF, EA, EB, LEV = 4, 24, 8, 128
DEV, CAP, ROWS = 128, 12, 16
AUX, COLS, STATE = 1013, 768, 512
F32, BF16 = jnp.float32, jnp.bfloat16
VMEM = pltpu.VMEM
EXCHANGE_VMEM, TAIL_VMEM = 53, 44
GROUPS = ((0, 0, 64), (0, 64, 128), (1, 0, 64), (1, 64, 104), (1, 104, 128))
HALF, MAIN, REST = 512, 384, 128
TURN = 53
TURN_BACK = pow(TURN, -1, DEV)


def node_tables():
    nodes = np.array([-1.0, -1.0 / np.sqrt(5.0), 1.0 / np.sqrt(5.0), 1.0])
    quadrature = np.array([1.0 / 6.0, 5.0 / 6.0, 5.0 / 6.0, 1.0 / 6.0])
    products = np.array(
        [np.prod([nodes[i] - nodes[k] for k in range(4) if k != i]) for i in range(4)]
    )
    derivative = np.zeros((4, 4))
    for i in range(4):
        for k in range(4):
            if i != k:
                derivative[i, k] = products[i] / (products[k] * (nodes[i] - nodes[k]))
            else:
                derivative[i, i] = sum(1.0 / (nodes[i] - nodes[m]) for m in range(4) if m != i)
    return derivative.astype(np.float32), quadrature.astype(np.float32)


def section_tables():
    d, w = node_tables()
    s = np.arange(8)
    up, j = s // 4, s % 4
    rows = []
    for p in range(2):
        i = 2 * p + up
        rows += [-d[i, up], -d[i, 1 - up], -d[i, 2 + up], -d[i, 3 - up]]
    rows += [-d[j, (j - shift) % 4] for shift in range(4)]
    rows += [w[2 * p + up] * w[j] for p in range(2)]
    return [[float(v) for v in row] for row in rows]


def sublane(shape):
    return lax.broadcasted_iota(jnp.int32, shape, len(shape) - 2)


def turn(x, shift):
    return pltpu.roll(x, shift % 8, axis=x.ndim - 2)


def pack_tables(pick):
    row = lax.broadcasted_iota(jnp.int32, (512, 384), 0)
    lane = lax.broadcasted_iota(jnp.int32, (512, 384), 1)
    base, slot = row // ROWS * CAP, row % ROWS
    for part in range(3):
        pick[part, :, :384] = jnp.where((slot < CAP) & (lane == base + slot), 1.0, 0.0).astype(BF16)
        pick[part, :, 384:] = jnp.where((slot >= CAP) & (lane == base + slot - CAP + 4 * part), 1.0, 0.0).astype(BF16)


def pack_block(aux, pick, packed, block):
    lanes = slice(384 * block, 384 * block + 384)
    last = aux[HALF + MAIN :, lanes].astype(F32)
    last = jnp.concatenate([last, jnp.zeros((2 * HALF - AUX, 384), F32)], axis=0).astype(BF16)
    last = jnp.concatenate([aux[MAIN:HALF, lanes], last], axis=0)
    for part in range(3):
        low = 128 * part
        piece = jnp.concatenate([aux[low : low + 128, lanes], aux[HALF + low : HALF + low + 128, lanes]], axis=0)
        value = lax.dot_general(
            pick[part], jnp.concatenate([piece, last], axis=1), (((1,), (1,)), ((), ())), preferred_element_type=F32
        ).astype(BF16)
        for h in range(2):
            packed[h, 32 * block : 32 * block + 32, :, low : low + 128] = value[:, 128 * h : 128 * h + 128].reshape(
                32, ROWS, 128
            )


def section_rows(tab_ref, sec, mass, sums, sides, cells):
    sub = sublane((EB, 8, LEV))
    j = sub % 4
    low = sub < 4
    is0, is3 = j == 0, j == 3

    def spread_row(a, _):
        tab = [tab_ref[k] for k in range(14)]
        weight = [tab[12 + p] * mass[a, :, p] for p in range(2)]
        msum = []
        for p in range(2):
            t = weight[p] + turn(weight[p], 4)
            msum.append(1.0 / (t + turn(t, 7)))
        flow = [[weight[p] * sec[f, a, :, p] for p in range(2)] for f in range(2)]
        for f in range(NF + 1):
            if f < NF:
                x = [sec[f, a, :, p] for p in range(2)]
                xs = [turn(x[p], 4) for p in range(2)]
                value = []
                for p in range(2):
                    da = (
                        tab[4 * p] * x[0] + tab[4 * p + 1] * xs[0]
                        + tab[4 * p + 2] * x[1] + tab[4 * p + 3] * xs[1]
                    )
                    db = tab[8] * x[p]
                    for shift in range(1, 4):
                        moved = turn(x[p], shift)
                        moved = jnp.where(j >= shift, moved, turn(moved, 4))
                        db += tab[8 + shift] * moved
                    value.append(flow[0][p] * da + flow[1][p] * db)
                    t = weight[p] * x[p]
                    t = t + turn(t, 4)
                    t = (t + turn(t, 7)) * msum[p]
                    for b in range(EB):
                        for q in range(2):
                            cells[f, pl.ds(a * 32 + b * 4 + p * 2 + q, 1), :] = t[b, 2 * q : 2 * q + 1]
            else:
                value = weight
            for p in range(2):
                v = value[p]
                for up in range(2):
                    place = pl.ds(a * 4 + 2 * p + up, 1)
                    sides[0, f, place, :] = v[0, 4 * up : 4 * up + 1]
                    sides[1, f, place, :] = v[EB - 1, 4 * up + 3 : 4 * up + 4]
                none = jnp.zeros((1, 8, LEV), F32)
                after = jnp.concatenate([none, turn(v[:-1], 5)], axis=0)
                before = jnp.concatenate([turn(v[1:], 3), none], axis=0)
                sums[f, a, :, p] = v + jnp.where(is0, after, jnp.where(is3, before, 0.0))
        return 0

    lax.fori_loop(0, EA, spread_row, 0)

    def join_rows(a, _):
        for f in range(NF + 1):
            here, there = sums[f, a, :, 1], sums[f, a + 1, :, 0]
            sums[f, a, :, 1] = here + jnp.where(low, 0.0, turn(there, 4))
            sums[f, a + 1, :, 0] = there + jnp.where(low, turn(here, 4), 0.0)
        return 0

    lax.fori_loop(0, EA - 1, join_rows, 0)


def side_edges(sides, edge):
    row = lax.broadcasted_iota(jnp.int32, (EA * 4, LEV), 0)
    above, below = (row % 4 == 3) & (row < EA * 4 - 1), (row % 4 == 0) & (row > 0)
    for k in range(2):
        for f in range(NF + 1):
            v = sides[k, f]
            up, down = pltpu.roll(v, EA * 4 - 1, axis=0), pltpu.roll(v, 1, axis=0)
            edge[k, f] = (v + jnp.where(above, up, jnp.where(below, down, 0.0))).astype(BF16)


def side_terms(sides, f, a, p):
    sub = sublane((8, LEV))
    low, j = sub < 4, sub % 4
    rows = [
        jnp.where(low, sides[k, f, pl.ds(a * 4 + 2 * p, 1), :], sides[k, f, pl.ds(a * 4 + 2 * p + 1, 1), :])
        for k in range(2)
    ]
    return jnp.where(j == 0, rows[0], 0.0), jnp.where(j == 3, rows[1], 0.0)


def rim_rows(sums, sides, rim):
    low = sublane((8, LEV)) < 4
    for k, (a, p) in enumerate(((0, 0), (EA - 1, 1))):
        for f in range(NF + 1):
            left, right = side_terms(sides, f, a, p)
            rows = [sums[f, a, b, p] for b in range(EB)]
            rows[0] += left
            rows[-1] += right
            if p:
                rows = [turn(r, 4) for r in rows]
            packed = [jnp.where(low, rows[b], turn(rows[b + 1], 4)) for b in range(0, EB, 2)]
            rim[k, f * 32 : (f + 1) * 32] = jnp.concatenate(packed, axis=0).astype(BF16)


def close_rows(sums, sides, rim, sec):
    low = sublane((8, LEV)) < 4

    def rim_terms(k, f):
        keep = low if k == 0 else jnp.logical_not(low)
        terms = []
        for pair in range(EB // 2):
            row = f * 32 + pair * 8
            both = rim[k, row : row + 8].astype(F32)
            pieces = (both, turn(both, 4)) if k == 0 else (turn(both, 4), both)
            terms += [jnp.where(keep, piece, 0.0)[None] for piece in pieces]
        return jnp.concatenate(terms, axis=0)

    for k, (a, p) in enumerate(((0, 0), (EA - 1, 1))):
        for f in range(NF + 1):
            sums[f, a, :, p] += rim_terms(k, f)

    def close_row(a, _):
        for p in range(2):
            total = []
            for f in range(NF + 1):
                left, right = side_terms(sides, f, a, p)
                v = sums[f, a, :, p]
                total.append(jnp.concatenate([v[:1] + left[None], v[1:-1], v[-1:] + right[None]], axis=0))
            scale = section_step / total[NF]
            for f in range(NF):
                sec[f, a, :, p] += total[f] * scale
        return 0

    lax.fori_loop(0, EA, close_row, 0)


def find_places(owner_ref, mine, out):
    curve, x = mine
    owner = owner_ref[...]
    there = owner // 4
    rel = (
        (x - owner % 4) % 4
        + (curve // 8 - there // 8) % 4 * 4
        + (curve // 2 - there // 2) % 4 * 16
        + (curve - there) % 2 * 64
    )
    order = rel * TURN_BACK % DEV
    hits = jnp.where(sublane((DEV, COLS)) == order, 1.0, 0.0)
    lane = lax.broadcasted_iota(jnp.int32, (COLS, COLS), 1)
    before = jnp.where(sublane((COLS, COLS)) < lane, 1.0, 0.0).astype(BF16)
    earlier = jnp.dot(hits.astype(BF16), before, preferred_element_type=F32)
    slot = jnp.sum(hits * earlier, axis=0, keepdims=True)
    base = order.astype(F32) * ROWS
    part = (slot >= 4).astype(F32) + (slot >= 8).astype(F32)
    rows = [base + slot, base + CAP + slot - 4 * part, part]
    out[...] = jnp.transpose(jnp.concatenate(rows + [part] * 5, axis=0)).astype(jnp.int32)


def exchange_kernel(
    owner_hbm, aux_ref, prog_ref, mass_ref, win_ref, sec_out, early_out, aux_out,
    tab_ref, owner_ref,
    aux, pick, packed, sec, mass, sums, sides, cells, home, win, early, state, acc, places, edge, edge_in, rim, rim_in,
    aux_sem, load_sem, store_sem, self_sem, send_sem, recv_sem, edge_send, edge_recv, rim_send, rim_recv,
):
    curve, x = lax.axis_index("curve"), lax.axis_index("sub")
    y, z, core = curve // 8, curve // 2 % 4, curve % 2
    me = curve * 4 + x
    mesh = pl.DeviceIdType.MESH

    loads = [
        pltpu.make_async_copy(prog_ref, sec, load_sem.at[0]),
        pltpu.make_async_copy(mass_ref, mass, load_sem.at[1]),
        pltpu.make_async_copy(win_ref.at[pl.ds(0, STATE + HALF)], win, load_sem.at[2]),
        pltpu.make_async_copy(owner_hbm, owner_ref, load_sem.at[3]),
    ]
    slots = [pl.ds(384 * n, 384) for n in range(4)]
    aux_loads = [pltpu.make_async_copy(aux_ref.at[:, s], aux.at[:, s], aux_sem.at[n]) for n, s in enumerate(slots)]
    for load in aux_loads + loads:
        load.start()

    barrier = pltpu.get_barrier_semaphore()

    def greet(d, _):
        t = lax.rem(me + d, DEV)
        pl.semaphore_signal(barrier, inc=1, device_id={"curve": t // 4, "sub": lax.rem(t, 4)}, device_id_type=mesh)
        return 0

    lax.fori_loop(1, DEV, greet, 0)
    pack_tables(pick)
    for n in range(4):
        aux_loads[n].wait()
        pack_block(aux, pick, packed, n)
    pl.semaphore_wait(barrier, DEV - 1)

    own = [pltpu.make_async_copy(packed.at[h, me], home.at[h, 0], self_sem.at[h]) for h in range(2)]
    for copy in own:
        copy.start()

    def send_group(g):
        h, first, end = GROUPS[g]

        def send(o, _):
            rel = lax.rem(o * TURN, DEV)
            to_x = lax.rem(x + rel % 4, 4)
            to_curve = (
                lax.rem(y + rel // 4 % 4, 4) * 8 + lax.rem(z + rel // 16 % 4, 4) * 2 + lax.rem(core + rel // 64, 2)
            )
            pltpu.make_async_remote_copy(
                packed.at[h, to_curve * 4 + to_x], home.at[h, o], send_sem.at[g], recv_sem.at[g],
                device_id={"curve": to_curve, "sub": to_x}, device_id_type=mesh,
            ).start()
            return 0

        lax.fori_loop(max(1, first), end, send, 0)

    def group_copy(g):
        h, first, end = GROUPS[g]
        span = pl.ds(max(1, first), end - max(1, first))
        return pltpu.make_async_remote_copy(
            packed.at[h, span], home.at[h, span], send_sem.at[g], recv_sem.at[g],
            device_id={"curve": curve, "sub": x}, device_id_type=mesh,
        )

    def select_group(g):
        group_copy(g).wait_recv()
        h, first, end = GROUPS[g]
        if first == 0:
            own[h].wait()
        depth = (end - first) * ROWS

        def chunk(m, _):
            rows = pl.ds(m * 256, 256)
            lane = lax.broadcasted_iota(jnp.int32, (256, depth), 1) + first * ROWS

            def pick(k):
                return jnp.where(lane == places[rows, k : k + 1], 1.0, 0.0).astype(BF16)

            block = home[h, first:end].reshape(depth, MAIN)
            main = jnp.dot(pick(0), block, preferred_element_type=F32)
            rest = jnp.dot(pick(1), block, preferred_element_type=F32)
            part = places[rows, 2:3]
            rest = jnp.where(part == 0, rest[:, :128], jnp.where(part == 1, rest[:, 128:256], rest[:, 256:]))
            if first:
                main, rest = main + acc[rows, :MAIN], rest + acc[rows, MAIN:]
            if end < DEV:
                acc[rows, :MAIN], acc[rows, MAIN:] = main, rest
            elif h == 0:
                state[rows, STATE : STATE + MAIN], state[rows, STATE + MAIN :] = main.astype(BF16), rest.astype(BF16)
            else:
                aux_out[rows, :MAIN], aux_out[rows, MAIN:] = main.astype(BF16), rest.astype(BF16)
            return 0

        lax.fori_loop(0, COLS // 256, chunk, 0)

    def both_ways(src, dst, send, recv, axis, place, count):
        return [
            pltpu.make_async_remote_copy(
                src.at[k], dst.at[1 - k], send.at[k], recv.at[1 - k],
                device_id={axis: lax.rem(place + (1 if k else count - 1), count)}, device_id_type=mesh,
            )
            for k in range(2)
        ]

    def await_both(copies):
        for copy in copies:
            copy.wait_recv()

    send_group(0)
    send_group(1)
    loads[0].wait()
    loads[1].wait()
    sub = sublane((8, LEV))
    for k, row in enumerate(section_tables()):
        value = jnp.full((8, LEV), row[0], F32)
        for n in range(1, 8):
            value = jnp.where(sub == n, row[n], value)
        tab_ref[k] = value
    section_rows(tab_ref, sec, mass, sums, sides, cells)
    side_edges(sides, edge)
    edge_copies = both_ways(edge, edge_in, edge_send, edge_recv, "sub", x, 4)
    for copy in edge_copies:
        copy.start()
    send_group(2)

    for f in range(NF):
        state[:, f * LEV : (f + 1) * LEV] = cells[f].astype(BF16)
    loads[3].wait()
    find_places(owner_ref, (curve, x), places)
    select_group(0)

    await_both(edge_copies)
    sides[...] = edge_in[...].astype(F32)
    rim_rows(sums, sides, rim)
    rim_copies = both_ways(rim, rim_in, rim_send, rim_recv, "curve", curve, 32)
    for copy in rim_copies:
        copy.start()
    send_group(3)
    send_group(4)

    select_group(1)
    loads[2].wait()

    def early_tile(t, _):
        lanes = pl.ds(pl.multiple_of(t * 256, 256), 256)
        early[:, lanes] = jnp.dot(state[...], win[:, lanes], preferred_element_type=F32)
        return 0

    lax.fori_loop(0, early.shape[1] // 256, early_tile, 0)
    early_store = pltpu.make_async_copy(early, early_out, store_sem.at[0])
    early_store.start()
    await_both(rim_copies)
    close_rows(sums, sides, rim_in, sec)
    sec_store = pltpu.make_async_copy(sec, sec_out, store_sem.at[1])
    sec_store.start()
    for g in range(2, len(GROUPS)):
        select_group(g)
    for g in range(len(GROUPS)):
        group_copy(g).wait_send()
    for copy in edge_copies + rim_copies:
        copy.wait_send()
    early_store.wait()
    sec_store.wait()


def exchange(owner, aux_t, prog, mass, weight_in):
    hid = weight_in.shape[1]
    vm, hbm = pl.BlockSpec(memory_space=VMEM), pl.BlockSpec(memory_space=pl.ANY)
    dma = pltpu.SemaphoreType.DMA
    return pl.pallas_call(
        exchange_kernel,
        in_specs=[hbm] * 5,
        out_specs=[hbm, hbm, vm],
        out_shape=[
            jax.ShapeDtypeStruct(prog.shape, F32),
            jax.ShapeDtypeStruct((COLS, hid), F32),
            jax.ShapeDtypeStruct((COLS, HALF), BF16),
        ],
        scratch_shapes=[
            VMEM((14, 8, LEV), F32),
            VMEM(owner.shape, jnp.int32),
            VMEM(aux_t.shape, BF16),
            VMEM((3, 512, 768), BF16),
            VMEM((2, DEV, ROWS, MAIN), BF16),
            VMEM(prog.shape, F32),
            VMEM(mass.shape, F32),
            VMEM((NF + 1, EA, EB, 2, 8, LEV), F32),
            VMEM((2, NF + 1, EA * 4, LEV), F32),
            VMEM((NF, COLS, LEV), F32),
            VMEM((2, DEV, ROWS, MAIN), BF16),
            VMEM((STATE + HALF, hid), BF16),
            VMEM((COLS, hid), F32),
            VMEM((COLS, STATE + HALF), BF16),
            VMEM((COLS, HALF), F32),
            VMEM((COLS, 8), jnp.int32),
            VMEM((2, NF + 1, EA * 4, LEV), BF16),
            VMEM((2, NF + 1, EA * 4, LEV), BF16),
            VMEM((2, (NF + 1) * 32, LEV), BF16),
            VMEM((2, (NF + 1) * 32, LEV), BF16),
            dma((4,)), dma((4,)), dma((2,)), dma((2,)), dma((len(GROUPS),)), dma((len(GROUPS),)), dma((2,)), dma((2,)), dma((2,)), dma((2,)),
        ],
        compiler_params=pltpu.CompilerParams(
            collective_id=1, has_side_effects=True, vmem_limit_bytes=EXCHANGE_VMEM << 20
        ),
        cost_estimate=pl.CostEstimate(flops=10_000_000_000, bytes_accessed=40_000_000, transcendentals=0),
    )(owner, aux_t, prog, mass, weight_in)


def tail_kernel(aux_ref, early_ref, win_ref, bin_ref, wout_ref, bout_ref, sec_ref, out_ref, inc, spread):
    step, last = pl.program_id(0), pl.num_programs(0) - 1
    count = aux_ref.shape[0]

    def add_block():
        term = jnp.dot(spread[...], inc[...], preferred_element_type=F32)
        for f in range(NF):
            piece = term[:, f * LEV : (f + 1) * LEV].reshape(sec_ref.shape[1:])
            out_ref[f] = sec_ref[f] + piece

    def network_block():
        total = bout_ref[...]
        aux = aux_ref[:, : AUX - HALF]
        for n in range(2):
            lanes = slice(1024 * n, 1024 * n + 1024)
            h = early_ref[:, lanes] + bin_ref[:, lanes] + jnp.dot(aux, win_ref[STATE + HALF :, lanes], preferred_element_type=F32)
            h = (h / (1.0 + jnp.exp(-h))).astype(BF16)
            total = total + jnp.dot(h, wout_ref[lanes, :], preferred_element_type=F32)
        return total.astype(BF16)

    def keep(total):
        inc[...] = total

    @pl.when(step == 0)
    def _():
        row = lax.broadcasted_iota(jnp.int32, spread.shape, 0)
        cell = row // 16 * 4 + row // 8 % 2 * 2 + row % 4 // 2
        lane = lax.broadcasted_iota(jnp.int32, spread.shape, 1)
        spread[...] = jnp.where(lane == cell, 1.0, 0.0).astype(BF16)
        keep(network_block())

    @pl.when((step > 0) & (step < last))
    def _():
        add_block()
        keep(network_block())

    @pl.when(step == last)
    def _():
        add_block()


def tail(aux, early, weight_in, bias_in, weight_out, bias_out, sec):
    steps = 3
    count, rows_a = COLS // steps, EA // steps
    ahead, behind = lambda n: jnp.minimum(n, steps - 1), lambda n: jnp.maximum(n - 1, 0)
    whole = pl.BlockSpec(memory_space=VMEM)
    block = pl.BlockSpec((NF, rows_a, EB, 2, 8, LEV), lambda n: (0, behind(n), 0, 0, 0, 0))
    return pl.pallas_call(
        tail_kernel,
        grid=(steps + 1,),
        in_specs=[
            pl.BlockSpec((count, aux.shape[1]), lambda n: (ahead(n), 0)),
            pl.BlockSpec((count, early.shape[1]), lambda n: (ahead(n), 0)),
            whole,
            whole,
            whole,
            whole,
            block,
        ],
        out_specs=block,
        out_shape=jax.ShapeDtypeStruct(sec.shape, F32),
        scratch_shapes=[VMEM((count, STATE), BF16), VMEM((4 * count, count), BF16)],
        compiler_params=pltpu.CompilerParams(vmem_limit_bytes=TAIL_VMEM << 20),
        cost_estimate=pl.CostEstimate(flops=5_000_000_000, bytes_accessed=30_000_000, transcendentals=0),
    )(aux, early, weight_in, bias_in, weight_out, bias_out, sec)


def shards(prognostic, layer_mass, column_aux, group_owner, weight_in, bias_in, weight_out, bias_out):
    prog = prognostic.reshape(NF, EA, EB, 2, 8, LEV)
    mass = layer_mass.reshape(EA, EB, 2, 8, LEV)
    sec, early, aux = exchange(
        group_owner.reshape(1, COLS), column_aux.T, prog, mass, weight_in
    )
    out = tail(aux, early, weight_in, bias_in[None], weight_out, bias_out[None], sec)
    return out.reshape(prognostic.shape)


def solution(mesh):
    return jax.shard_map(
        shards,
        mesh=mesh,
        in_specs=(
            P(None, "curve", "sub", None, None, None),
            P("curve", "sub", None, None, None),
            P(("curve", "sub"), None),
            P(("curve", "sub"), None),
            P(),
            P(),
            P(),
            P(),
        ),
        out_specs=P(None, "curve", "sub", None, None, None),
        check_vma=False,
    )
```

```python
import jax
import jax.numpy as jnp
import numpy as np
from jax import lax
from jax.experimental import pallas as pl
from jax.experimental.pallas import tpu as pltpu
from jax.sharding import PartitionSpec as P

section_step = 0.1
NF, EA, EB, LEV = 4, 24, 8, 128
DEV, CAP, ROWS = 128, 12, 16
AUX, COLS, STATE = 1013, 768, 512
F32, BF16 = jnp.float32, jnp.bfloat16
VMEM = pltpu.VMEM
EXCHANGE_VMEM, TAIL_VMEM = 53, 44
GROUPS = ((0, 0, 64), (0, 64, 128), (1, 0, 64), (1, 64, 112), (1, 112, 128))
HALF, MAIN, REST = 512, 384, 128
TURN = 53
TURN_BACK = pow(TURN, -1, DEV)


def node_tables():
    nodes = np.array([-1.0, -1.0 / np.sqrt(5.0), 1.0 / np.sqrt(5.0), 1.0])
    quadrature = np.array([1.0 / 6.0, 5.0 / 6.0, 5.0 / 6.0, 1.0 / 6.0])
    products = np.array(
        [np.prod([nodes[i] - nodes[k] for k in range(4) if k != i]) for i in range(4)]
    )
    derivative = np.zeros((4, 4))
    for i in range(4):
        for k in range(4):
            if i != k:
                derivative[i, k] = products[i] / (products[k] * (nodes[i] - nodes[k]))
            else:
                derivative[i, i] = sum(1.0 / (nodes[i] - nodes[m]) for m in range(4) if m != i)
    return derivative.astype(np.float32), quadrature.astype(np.float32)


def section_tables():
    d, w = node_tables()
    s = np.arange(8)
    up, j = s // 4, s % 4
    rows = []
    for p in range(2):
        i = 2 * p + up
        rows += [-d[i, up], -d[i, 1 - up], -d[i, 2 + up], -d[i, 3 - up]]
    rows += [-d[j, (j - shift) % 4] for shift in range(4)]
    rows += [w[2 * p + up] * w[j] for p in range(2)]
    return [[float(v) for v in row] for row in rows]


def sublane(shape):
    return lax.broadcasted_iota(jnp.int32, shape, len(shape) - 2)


def turn(x, shift):
    return pltpu.roll(x, shift % 8, axis=x.ndim - 2)


def pack_tables(pick):
    row = lax.broadcasted_iota(jnp.int32, (512, 384), 0)
    lane = lax.broadcasted_iota(jnp.int32, (512, 384), 1)
    base, slot = row // ROWS * CAP, row % ROWS
    for part in range(3):
        pick[part, :, :384] = jnp.where((slot < CAP) & (lane == base + slot), 1.0, 0.0).astype(BF16)
        pick[part, :, 384:] = jnp.where((slot >= CAP) & (lane == base + slot - CAP + 4 * part), 1.0, 0.0).astype(BF16)


def pack_block(aux, pick, packed, block):
    lanes = slice(384 * block, 384 * block + 384)
    last = aux[HALF + MAIN :, lanes].astype(F32)
    last = jnp.concatenate([last, jnp.zeros((2 * HALF - AUX, 384), F32)], axis=0).astype(BF16)
    last = jnp.concatenate([aux[MAIN:HALF, lanes], last], axis=0)
    for part in range(3):
        low = 128 * part
        piece = jnp.concatenate([aux[low : low + 128, lanes], aux[HALF + low : HALF + low + 128, lanes]], axis=0)
        value = lax.dot_general(
            pick[part], jnp.concatenate([piece, last], axis=1), (((1,), (1,)), ((), ())), preferred_element_type=F32
        ).astype(BF16)
        for h in range(2):
            packed[h, 32 * block : 32 * block + 32, :, low : low + 128] = value[:, 128 * h : 128 * h + 128].reshape(
                32, ROWS, 128
            )


def section_rows(tab_ref, sec, mass, sums, sides, cells):
    sub = sublane((EB, 8, LEV))
    j = sub % 4
    low = sub < 4
    is0, is3 = j == 0, j == 3

    def spread_row(a, _):
        tab = [tab_ref[k] for k in range(14)]
        weight = [tab[12 + p] * mass[a, :, p] for p in range(2)]
        msum = []
        for p in range(2):
            t = weight[p] + turn(weight[p], 4)
            msum.append(1.0 / (t + turn(t, 7)))
        flow = [[weight[p] * sec[f, a, :, p] for p in range(2)] for f in range(2)]
        for f in range(NF + 1):
            if f < NF:
                x = [sec[f, a, :, p] for p in range(2)]
                xs = [turn(x[p], 4) for p in range(2)]
                value = []
                for p in range(2):
                    da = (
                        tab[4 * p] * x[0] + tab[4 * p + 1] * xs[0]
                        + tab[4 * p + 2] * x[1] + tab[4 * p + 3] * xs[1]
                    )
                    db = tab[8] * x[p]
                    for shift in range(1, 4):
                        moved = turn(x[p], shift)
                        moved = jnp.where(j >= shift, moved, turn(moved, 4))
                        db += tab[8 + shift] * moved
                    value.append(flow[0][p] * da + flow[1][p] * db)
                    t = weight[p] * x[p]
                    t = t + turn(t, 4)
                    t = (t + turn(t, 7)) * msum[p]
                    for b in range(EB):
                        for q in range(2):
                            cells[f, pl.ds(a * 32 + b * 4 + p * 2 + q, 1), :] = t[b, 2 * q : 2 * q + 1]
            else:
                value = weight
            for p in range(2):
                v = value[p]
                for up in range(2):
                    place = pl.ds(a * 4 + 2 * p + up, 1)
                    sides[0, f, place, :] = v[0, 4 * up : 4 * up + 1]
                    sides[1, f, place, :] = v[EB - 1, 4 * up + 3 : 4 * up + 4]
                none = jnp.zeros((1, 8, LEV), F32)
                after = jnp.concatenate([none, turn(v[:-1], 5)], axis=0)
                before = jnp.concatenate([turn(v[1:], 3), none], axis=0)
                sums[f, a, :, p] = v + jnp.where(is0, after, jnp.where(is3, before, 0.0))
        return 0

    lax.fori_loop(0, EA, spread_row, 0)

    def join_rows(a, _):
        for f in range(NF + 1):
            here, there = sums[f, a, :, 1], sums[f, a + 1, :, 0]
            sums[f, a, :, 1] = here + jnp.where(low, 0.0, turn(there, 4))
            sums[f, a + 1, :, 0] = there + jnp.where(low, turn(here, 4), 0.0)
        return 0

    lax.fori_loop(0, EA - 1, join_rows, 0)


def side_edges(sides, edge):
    row = lax.broadcasted_iota(jnp.int32, (EA * 4, LEV), 0)
    above, below = (row % 4 == 3) & (row < EA * 4 - 1), (row % 4 == 0) & (row > 0)
    for k in range(2):
        for f in range(NF + 1):
            v = sides[k, f]
            up, down = pltpu.roll(v, EA * 4 - 1, axis=0), pltpu.roll(v, 1, axis=0)
            edge[k, f] = (v + jnp.where(above, up, jnp.where(below, down, 0.0))).astype(BF16)


def side_terms(sides, f, a, p):
    sub = sublane((8, LEV))
    low, j = sub < 4, sub % 4
    rows = [
        jnp.where(low, sides[k, f, pl.ds(a * 4 + 2 * p, 1), :], sides[k, f, pl.ds(a * 4 + 2 * p + 1, 1), :])
        for k in range(2)
    ]
    return jnp.where(j == 0, rows[0], 0.0), jnp.where(j == 3, rows[1], 0.0)


def rim_rows(sums, sides, rim):
    low = sublane((8, LEV)) < 4
    for k, (a, p) in enumerate(((0, 0), (EA - 1, 1))):
        for f in range(NF + 1):
            left, right = side_terms(sides, f, a, p)
            rows = [sums[f, a, b, p] for b in range(EB)]
            rows[0] += left
            rows[-1] += right
            if p:
                rows = [turn(r, 4) for r in rows]
            packed = [jnp.where(low, rows[b], turn(rows[b + 1], 4)) for b in range(0, EB, 2)]
            rim[k, f * 32 : (f + 1) * 32] = jnp.concatenate(packed, axis=0).astype(BF16)


def close_rows(sums, sides, rim, sec):
    low = sublane((8, LEV)) < 4

    def rim_terms(k, f):
        keep = low if k == 0 else jnp.logical_not(low)
        terms = []
        for pair in range(EB // 2):
            row = f * 32 + pair * 8
            both = rim[k, row : row + 8].astype(F32)
            pieces = (both, turn(both, 4)) if k == 0 else (turn(both, 4), both)
            terms += [jnp.where(keep, piece, 0.0)[None] for piece in pieces]
        return jnp.concatenate(terms, axis=0)

    for k, (a, p) in enumerate(((0, 0), (EA - 1, 1))):
        for f in range(NF + 1):
            sums[f, a, :, p] += rim_terms(k, f)

    def close_row(a, _):
        for p in range(2):
            total = []
            for f in range(NF + 1):
                left, right = side_terms(sides, f, a, p)
                v = sums[f, a, :, p]
                total.append(jnp.concatenate([v[:1] + left[None], v[1:-1], v[-1:] + right[None]], axis=0))
            scale = section_step / total[NF]
            for f in range(NF):
                sec[f, a, :, p] += total[f] * scale
        return 0

    lax.fori_loop(0, EA, close_row, 0)


def find_places(owner_ref, mine, out):
    curve, x = mine
    owner = owner_ref[...]
    there = owner // 4
    rel = (
        (x - owner % 4) % 4
        + (curve // 8 - there // 8) % 4 * 4
        + (curve // 2 - there // 2) % 4 * 16
        + (curve - there) % 2 * 64
    )
    order = rel * TURN_BACK % DEV
    hits = jnp.where(sublane((DEV, COLS)) == order, 1.0, 0.0)
    lane = lax.broadcasted_iota(jnp.int32, (COLS, COLS), 1)
    before = jnp.where(sublane((COLS, COLS)) < lane, 1.0, 0.0).astype(BF16)
    earlier = jnp.dot(hits.astype(BF16), before, preferred_element_type=F32)
    slot = jnp.sum(hits * earlier, axis=0, keepdims=True)
    base = order.astype(F32) * ROWS
    part = (slot >= 4).astype(F32) + (slot >= 8).astype(F32)
    rows = [base + slot, base + CAP + slot - 4 * part, part]
    out[...] = jnp.transpose(jnp.concatenate(rows + [part] * 5, axis=0)).astype(jnp.int32)


def exchange_kernel(
    owner_hbm, aux_ref, prog_ref, mass_ref, win_ref, sec_out, early_out, aux_out,
    tab_ref, owner_ref,
    aux, pick, packed, sec, mass, sums, sides, cells, home, win, early, state, acc, places, edge, edge_in, rim, rim_in,
    aux_sem, load_sem, store_sem, self_sem, send_sem, recv_sem, edge_send, edge_recv, rim_send, rim_recv,
):
    curve, x = lax.axis_index("curve"), lax.axis_index("sub")
    y, z, core = curve // 8, curve // 2 % 4, curve % 2
    me = curve * 4 + x
    mesh = pl.DeviceIdType.MESH

    loads = [
        pltpu.make_async_copy(prog_ref, sec, load_sem.at[0]),
        pltpu.make_async_copy(mass_ref, mass, load_sem.at[1]),
        pltpu.make_async_copy(win_ref.at[pl.ds(0, STATE + HALF)], win, load_sem.at[2]),
        pltpu.make_async_copy(owner_hbm, owner_ref, load_sem.at[3]),
    ]
    slots = [pl.ds(384 * n, 384) for n in range(4)]
    aux_loads = [pltpu.make_async_copy(aux_ref.at[:, s], aux.at[:, s], aux_sem.at[n]) for n, s in enumerate(slots)]
    for load in aux_loads + loads:
        load.start()

    barrier = pltpu.get_barrier_semaphore()

    def greet(d, _):
        t = lax.rem(me + d, DEV)
        pl.semaphore_signal(barrier, inc=1, device_id={"curve": t // 4, "sub": lax.rem(t, 4)}, device_id_type=mesh)
        return 0

    lax.fori_loop(1, DEV, greet, 0)
    pack_tables(pick)
    for n in range(4):
        aux_loads[n].wait()
        pack_block(aux, pick, packed, n)
    pl.semaphore_wait(barrier, DEV - 1)

    own = [pltpu.make_async_copy(packed.at[h, me], home.at[h, 0], self_sem.at[h]) for h in range(2)]
    for copy in own:
        copy.start()

    def send_group(g):
        h, first, end = GROUPS[g]

        def send(o, _):
            rel = lax.rem(o * TURN, DEV)
            to_x = lax.rem(x + rel % 4, 4)
            to_curve = (
                lax.rem(y + rel // 4 % 4, 4) * 8 + lax.rem(z + rel // 16 % 4, 4) * 2 + lax.rem(core + rel // 64, 2)
            )
            pltpu.make_async_remote_copy(
                packed.at[h, to_curve * 4 + to_x], home.at[h, o], send_sem.at[g], recv_sem.at[g],
                device_id={"curve": to_curve, "sub": to_x}, device_id_type=mesh,
            ).start()
            return 0

        lax.fori_loop(max(1, first), end, send, 0)

    def group_copy(g):
        h, first, end = GROUPS[g]
        span = pl.ds(max(1, first), end - max(1, first))
        return pltpu.make_async_remote_copy(
            packed.at[h, span], home.at[h, span], send_sem.at[g], recv_sem.at[g],
            device_id={"curve": curve, "sub": x}, device_id_type=mesh,
        )

    def select_group(g):
        group_copy(g).wait_recv()
        h, first, end = GROUPS[g]
        if first == 0:
            own[h].wait()
        depth = (end - first) * ROWS

        def chunk(m, _):
            rows = pl.ds(m * 256, 256)
            lane = lax.broadcasted_iota(jnp.int32, (256, depth), 1) + first * ROWS

            def pick(k):
                return jnp.where(lane == places[rows, k : k + 1], 1.0, 0.0).astype(BF16)

            block = home[h, first:end].reshape(depth, MAIN)
            main = jnp.dot(pick(0), block, preferred_element_type=F32)
            rest = jnp.dot(pick(1), block, preferred_element_type=F32)
            part = places[rows, 2:3]
            rest = jnp.where(part == 0, rest[:, :128], jnp.where(part == 1, rest[:, 128:256], rest[:, 256:]))
            if first:
                main, rest = main + acc[rows, :MAIN], rest + acc[rows, MAIN:]
            if end < DEV:
                acc[rows, :MAIN], acc[rows, MAIN:] = main, rest
            elif h == 0:
                state[rows, STATE : STATE + MAIN], state[rows, STATE + MAIN :] = main.astype(BF16), rest.astype(BF16)
            else:
                aux_out[rows, :MAIN], aux_out[rows, MAIN:] = main.astype(BF16), rest.astype(BF16)
            return 0

        lax.fori_loop(0, COLS // 256, chunk, 0)

    def both_ways(src, dst, send, recv, axis, place, count):
        return [
            pltpu.make_async_remote_copy(
                src.at[k], dst.at[1 - k], send.at[k], recv.at[1 - k],
                device_id={axis: lax.rem(place + (1 if k else count - 1), count)}, device_id_type=mesh,
            )
            for k in range(2)
        ]

    def await_both(copies):
        for copy in copies:
            copy.wait_recv()

    send_group(0)
    send_group(1)
    loads[0].wait()
    loads[1].wait()
    sub = sublane((8, LEV))
    for k, row in enumerate(section_tables()):
        value = jnp.full((8, LEV), row[0], F32)
        for n in range(1, 8):
            value = jnp.where(sub == n, row[n], value)
        tab_ref[k] = value
    section_rows(tab_ref, sec, mass, sums, sides, cells)
    side_edges(sides, edge)
    edge_copies = both_ways(edge, edge_in, edge_send, edge_recv, "sub", x, 4)
    for copy in edge_copies:
        copy.start()
    send_group(2)

    for f in range(NF):
        state[:, f * LEV : (f + 1) * LEV] = cells[f].astype(BF16)
    loads[3].wait()
    find_places(owner_ref, (curve, x), places)
    select_group(0)

    await_both(edge_copies)
    sides[...] = edge_in[...].astype(F32)
    rim_rows(sums, sides, rim)
    rim_copies = both_ways(rim, rim_in, rim_send, rim_recv, "curve", curve, 32)
    for copy in rim_copies:
        copy.start()
    send_group(3)
    send_group(4)

    select_group(1)
    loads[2].wait()

    def early_tile(t, _):
        lanes = pl.ds(pl.multiple_of(t * 256, 256), 256)
        early[:, lanes] = jnp.dot(state[...], win[:, lanes], preferred_element_type=F32)
        return 0

    lax.fori_loop(0, early.shape[1] // 256, early_tile, 0)
    early_store = pltpu.make_async_copy(early, early_out, store_sem.at[0])
    early_store.start()
    await_both(rim_copies)
    close_rows(sums, sides, rim_in, sec)
    sec_store = pltpu.make_async_copy(sec, sec_out, store_sem.at[1])
    sec_store.start()
    for g in range(2, len(GROUPS)):
        select_group(g)
    for g in range(len(GROUPS)):
        group_copy(g).wait_send()
    for copy in edge_copies + rim_copies:
        copy.wait_send()
    early_store.wait()
    sec_store.wait()


def exchange(owner, aux_t, prog, mass, weight_in):
    hid = weight_in.shape[1]
    vm, hbm = pl.BlockSpec(memory_space=VMEM), pl.BlockSpec(memory_space=pl.ANY)
    dma = pltpu.SemaphoreType.DMA
    return pl.pallas_call(
        exchange_kernel,
        in_specs=[hbm] * 5,
        out_specs=[hbm, hbm, vm],
        out_shape=[
            jax.ShapeDtypeStruct(prog.shape, F32),
            jax.ShapeDtypeStruct((COLS, hid), F32),
            jax.ShapeDtypeStruct((COLS, HALF), BF16),
        ],
        scratch_shapes=[
            VMEM((14, 8, LEV), F32),
            VMEM(owner.shape, jnp.int32),
            VMEM(aux_t.shape, BF16),
            VMEM((3, 512, 768), BF16),
            VMEM((2, DEV, ROWS, MAIN), BF16),
            VMEM(prog.shape, F32),
            VMEM(mass.shape, F32),
            VMEM((NF + 1, EA, EB, 2, 8, LEV), F32),
            VMEM((2, NF + 1, EA * 4, LEV), F32),
            VMEM((NF, COLS, LEV), F32),
            VMEM((2, DEV, ROWS, MAIN), BF16),
            VMEM((STATE + HALF, hid), BF16),
            VMEM((COLS, hid), F32),
            VMEM((COLS, STATE + HALF), BF16),
            VMEM((COLS, HALF), F32),
            VMEM((COLS, 8), jnp.int32),
            VMEM((2, NF + 1, EA * 4, LEV), BF16),
            VMEM((2, NF + 1, EA * 4, LEV), BF16),
            VMEM((2, (NF + 1) * 32, LEV), BF16),
            VMEM((2, (NF + 1) * 32, LEV), BF16),
            dma((4,)), dma((4,)), dma((2,)), dma((2,)), dma((len(GROUPS),)), dma((len(GROUPS),)), dma((2,)), dma((2,)), dma((2,)), dma((2,)),
        ],
        compiler_params=pltpu.CompilerParams(
            collective_id=1, has_side_effects=True, vmem_limit_bytes=EXCHANGE_VMEM << 20
        ),
        cost_estimate=pl.CostEstimate(flops=10_000_000_000, bytes_accessed=40_000_000, transcendentals=0),
    )(owner, aux_t, prog, mass, weight_in)


def tail_kernel(aux_ref, early_ref, win_ref, bin_ref, wout_ref, bout_ref, sec_ref, out_ref, inc, spread):
    step, last = pl.program_id(0), pl.num_programs(0) - 1
    count = aux_ref.shape[0]

    def add_block():
        term = jnp.dot(spread[...], inc[...], preferred_element_type=F32)
        for f in range(NF):
            piece = term[:, f * LEV : (f + 1) * LEV].reshape(sec_ref.shape[1:])
            out_ref[f] = sec_ref[f] + piece

    def network_block():
        total = bout_ref[...]
        aux = aux_ref[:, : AUX - HALF]
        for n in range(1):
            lanes = slice(2048 * n, 2048 * n + 2048)
            h = early_ref[:, lanes] + bin_ref[:, lanes] + jnp.dot(aux, win_ref[STATE + HALF :, lanes], preferred_element_type=F32)
            h = (h / (1.0 + jnp.exp(-h))).astype(BF16)
            total = total + jnp.dot(h, wout_ref[lanes, :], preferred_element_type=F32)
        return total.astype(BF16)

    def keep(total):
        inc[...] = total

    @pl.when(step == 0)
    def _():
        row = lax.broadcasted_iota(jnp.int32, spread.shape, 0)
        cell = row // 16 * 4 + row // 8 % 2 * 2 + row % 4 // 2
        lane = lax.broadcasted_iota(jnp.int32, spread.shape, 1)
        spread[...] = jnp.where(lane == cell, 1.0, 0.0).astype(BF16)
        keep(network_block())

    @pl.when((step > 0) & (step < last))
    def _():
        add_block()
        keep(network_block())

    @pl.when(step == last)
    def _():
        add_block()


def tail(aux, early, weight_in, bias_in, weight_out, bias_out, sec):
    steps = 3
    count, rows_a = COLS // steps, EA // steps
    ahead, behind = lambda n: jnp.minimum(n, steps - 1), lambda n: jnp.maximum(n - 1, 0)
    whole = pl.BlockSpec(memory_space=VMEM)
    block = pl.BlockSpec((NF, rows_a, EB, 2, 8, LEV), lambda n: (0, behind(n), 0, 0, 0, 0))
    return pl.pallas_call(
        tail_kernel,
        grid=(steps + 1,),
        in_specs=[
            pl.BlockSpec((count, aux.shape[1]), lambda n: (ahead(n), 0)),
            pl.BlockSpec((count, early.shape[1]), lambda n: (ahead(n), 0)),
            whole,
            whole,
            whole,
            whole,
            block,
        ],
        out_specs=block,
        out_shape=jax.ShapeDtypeStruct(sec.shape, F32),
        scratch_shapes=[VMEM((count, STATE), BF16), VMEM((4 * count, count), BF16)],
        compiler_params=pltpu.CompilerParams(vmem_limit_bytes=TAIL_VMEM << 20),
        cost_estimate=pl.CostEstimate(flops=5_000_000_000, bytes_accessed=30_000_000, transcendentals=0),
    )(aux, early, weight_in, bias_in, weight_out, bias_out, sec)


def shards(prognostic, layer_mass, column_aux, group_owner, weight_in, bias_in, weight_out, bias_out):
    prog = prognostic.reshape(NF, EA, EB, 2, 8, LEV)
    mass = layer_mass.reshape(EA, EB, 2, 8, LEV)
    sec, early, aux = exchange(
        group_owner.reshape(1, COLS), column_aux.T, prog, mass, weight_in
    )
    out = tail(aux, early, weight_in, bias_in[None], weight_out, bias_out[None], sec)
    return out.reshape(prognostic.shape)


def solution(mesh):
    return jax.shard_map(
        shards,
        mesh=mesh,
        in_specs=(
            P(None, "curve", "sub", None, None, None),
            P("curve", "sub", None, None, None),
            P(("curve", "sub"), None),
            P(("curve", "sub"), None),
            P(),
            P(),
            P(),
            P(),
        ),
        out_specs=P(None, "curve", "sub", None, None, None),
        check_vma=False,
    )
```
